32 devices in a mesh: dp: 2 (over y), member: 4 (over z), mp: 4 (over x, core).
Axes of the slice: x: 2, y: 2, z: 4, core: 2. Of those that a mesh axis runs over, the one named last changes fastest.
Arguments:
- hidden: bfloat16 [256, 4096], P('dp', ('member', 'mp')), may hold values from -9 to 9
- w_in: bfloat16 [4, 4096, 4096], P('member', 'dp', 'mp'), may hold values from -0.09375 to 0.09375
- w_out: bfloat16 [4, 4096, 4096], P('member', 'mp', 'dp'), may hold values from -0.09375 to 0.09375
- score_vec: float32 [4, 4096], P('member'), may hold values from -1 to 1
- lengths: int32 [2, 4], P('dp'), may hold values from 1 to 64, 128 in all within a row
- reward_offset: int32 [2, 4], P('dp'), may hold values from 0 to 63
- seq_weight: float32 [2, 4], P('dp'), may hold values from -4 to 4
Outputs:
- penalized: float32 [2, 4], P('dp')
- grad_hidden: float32 [256, 4096], P('dp', ('member', 'mp'))
- grad_in: float32 [4, 4096, 4096], P('member', 'dp', 'mp')
- grad_out: float32 [4, 4096, 4096], P('member', 'mp', 'dp')
The draws below stay inside these ranges and needn't reach their ends.
Inputs may be any that keep to these rules, and one draw needn't show every extreme that they name: Each row of lengths sums to 128, and its largest entry is exactly 64.
All inputs are finite; a program needn't handle non-finite values.
Results may differ from the reference program's by a relative error of at most 0.018.
Values may be sent and summed in bfloat16 or wider, within the bound.
A program may use at most 64 MiB of HBM per device.

```python
import math
import jax
import jax.numpy as jnp
import numpy as np
from jax import lax

D = 4096
FF = 4096
SLAB = 128
SEQS = 4
MOST = 64
HEADS = 4
SLABS = 2
TOKENS = 256


def shared_direction(key):
    picks = jax.random.randint(jax.random.fold_in(key, 7101), (D,), 0, 2)
    return (picks * 2 - 1).astype(jnp.float32)


def draw_hidden(key, part):
    direction = shared_direction(key)
    keys = jax.random.split(jax.random.fold_in(key, 7202), 4)
    noise = jnp.clip(jax.random.normal(keys[0], (TOKENS, D), jnp.float32), -4.0, 4.0) * 0.6
    magnitude = jax.random.uniform(keys[1], (TOKENS,), jnp.float32, 0.7, 1.0)
    signs = (jax.random.randint(keys[2], (TOKENS,), 0, 2) * 2 - 1).astype(jnp.float32)
    pairing = jax.random.permutation(keys[3], SLABS)
    slab_of = jnp.arange(TOKENS, dtype=jnp.int32) // SLAB
    block_of = jnp.arange(D, dtype=jnp.int32) // (D // SLABS)
    paired = pairing[slab_of][:, None] == block_of[None, :]
    boost = jnp.where(paired, 3.0, 1.0)
    values = noise * boost + (signs * magnitude)[:, None] * direction[None, :]
    return values.astype(jnp.bfloat16)


def draw_score_vec(key, part):
    direction = shared_direction(key)
    keys = jax.random.split(jax.random.fold_in(key, 7303), 3)
    noise = jnp.clip(jax.random.normal(keys[0], (HEADS, D), jnp.float32), -4.0, 4.0)
    magnitude = jax.random.uniform(keys[1], (HEADS,), jnp.float32, 0.4, 1.0)
    signs = (jax.random.randint(keys[2], (HEADS,), 0, 2) * 2 - 1).astype(jnp.float32)
    values = (signs * magnitude)[:, None] * direction[None, :] + 0.5 * noise
    return (values * (8.0 / D)).astype(jnp.float32)


def touch_ends(drawn, key, smallest, high):
    longest = drawn.shape.index(max(drawn.shape))
    spots = []
    for shift in (0, 1):
        where = [jax.random.randint(jax.random.fold_in(key, axis), (), 0, length) for axis, length in enumerate(drawn.shape)]
        where[longest] = (where[longest] + shift) % drawn.shape[longest]
        spots.append(tuple(where))
    return drawn.at[spots[0]].set(smallest).at[spots[1]].set(high)


def shard_levels(own_key, dims, cuts, low, top_value):
    def one(position, shards_of):
        heights = jax.random.uniform(jax.random.fold_in(jax.random.fold_in(own_key, 6), position), (shards_of,), jnp.float32, low / len(cuts), top_value / len(cuts))
        return jnp.repeat(jnp.exp(heights), dims[position] // shards_of).reshape((-1,) + (1,) * (len(dims) - position - 1))

    loudness = one(*cuts[0])
    for cut in cuts[1:]:
        loudness = loudness * one(*cut)
    return loudness


def length_profile(number_of, total, bound, slope):
    portions = [(1 << 20) // math.isqrt(standing ** slope) + 1 for standing in range(2, number_of + 1)]
    spare, holding = total - bound - (number_of - 1), [1] * (number_of - 1)
    while spare > 0:
        candidates = [i for i in range(number_of - 1) if holding[i] < bound]
        whole, left = sum([portions[i] for i in candidates]), spare
        for i in candidates:
            extra = min(bound - holding[i], max(1, left * portions[i] // whole), spare)
            holding[i] = holding[i] + extra
            spare = spare - extra
    return np.array([bound] + holding)


def uneven_parts(rng, count, total, bound, lean):
    if count == 2:
        one = jax.random.randint(rng, (), max(1, total - bound), min(bound, total - 1) + 1)
        return jnp.stack([one, total - one])
    sizes = jnp.asarray(length_profile(count, total, bound, lean), jnp.int32)
    twos = (count - 1) // 2
    source_of, receiver = sizes[1:1 + 2 * twos:2], sizes[2:2 + 2 * twos:2]
    slack = jnp.minimum(source_of - 1, bound - receiver)
    moved = jax.random.randint(jax.random.fold_in(rng, 1), (twos,), 0, 1 << 20) % (slack + 1)
    sizes = sizes.at[1:1 + 2 * twos:2].set(source_of - moved).at[2:2 + 2 * twos:2].set(receiver + moved)
    return sizes[jax.random.permutation(jax.random.fold_in(rng, 2), count)]


def bell_draw(stream_key, extent, width, most, cuts=(), kind=jnp.bfloat16):
    result = width * jax.random.normal(stream_key, extent, jnp.float32)
    if cuts:
        result = result * shard_levels(stream_key, extent, cuts, -0.22, 0.18)
    return jnp.clip(result, -most, most).astype(kind)


def setup_inputs(seed: int = 0) -> dict:
    arg_keys = jax.random.split(jax.random.key(seed), 8)
    return {
        "hidden": draw_hidden(jax.random.fold_in(arg_keys[7], 71), 0),
        "w_in": bell_draw(arg_keys[1], (HEADS, D, FF), D ** -0.5, 0.09375, ((0, 4), (1, 2), (2, 4))),
        "w_out": bell_draw(arg_keys[2], (HEADS, FF, D), FF ** -0.5, 0.09375, ((0, 4), (1, 4), (2, 2))),
        "score_vec": draw_score_vec(jax.random.fold_in(arg_keys[7], 71), 0),
        "lengths": jax.vmap(lambda own: uneven_parts(own, SEQS, SLAB, MOST, 2))(jax.random.split(arg_keys[4], SLABS)).reshape((SLABS, SEQS)).astype(jnp.int32),
        "reward_offset": touch_ends(jax.random.randint(arg_keys[5], (SLABS, SEQS), 0, MOST), jax.random.fold_in(arg_keys[5], 1), 0, MOST - 1).astype(jnp.int32),
        "seq_weight": bell_draw(arg_keys[6], (SLABS, SEQS), 1.0, 4.0, ((0, 2),), jnp.float32),
    }


PENALTY = 0.5
SPREAD_FLOOR = 0.25
EPSILON = 1e-05
PRECISE = lax.Precision.HIGHEST

def pooling(lengths, offsets, row_count):
    lengths = lengths.astype(jnp.int32)
    seq_ends = jnp.cumsum(lengths).astype(jnp.int32)
    seq_starts = seq_ends - lengths
    target = seq_starts + offsets.astype(jnp.int32) % lengths
    places = jnp.arange(row_count, dtype=jnp.int32)[:, None]
    inside = jnp.logical_and(places >= seq_starts[None, :], places < seq_ends[None, :])
    marked = places == target[None, :]
    return inside.astype(jnp.float32) / lengths.astype(jnp.float32)[None, :] + marked.astype(jnp.float32)

def silu_slope(gate_in):
    sigmoided = jax.nn.sigmoid(gate_in)
    return sigmoided * (1.0 + gate_in * (1.0 - sigmoided))

def slab_forward(slab_rows, w_first, w_second, vector, pooler):
    gate_in = jnp.dot(slab_rows, w_first, preferred_element_type=jnp.float32)
    activated = jax.nn.silu(gate_in).astype(jnp.bfloat16)
    combined = slab_rows.astype(jnp.float32) + jnp.dot(activated, w_second, preferred_element_type=jnp.float32)
    inverse = lax.rsqrt(lax.optimization_barrier(jnp.mean(combined * combined, axis=1)) + EPSILON)
    scores = jnp.dot(combined, vector, precision=PRECISE) * inverse
    rewards = jnp.dot(scores, pooler, precision=PRECISE)
    return (gate_in, activated, combined, inverse, scores, rewards)

def reference(hidden, w_in, w_out, score_vec, lengths, reward_offset, seq_weight):
    slab_count = lengths.shape[0]
    head_count = w_in.shape[0]
    row_count = hidden.shape[0] // slab_count
    feature_count = hidden.shape[1]
    slab_blocks = hidden.reshape(slab_count, row_count, feature_count)
    poolers = jax.vmap(lambda seq_len, seq_off: pooling(seq_len, seq_off, row_count))(lengths, reward_offset)
    head_ids = jnp.arange(head_count, dtype=jnp.int32)

    def forward(head_id):

        def reward_of(entry):
            return slab_forward(entry[0], w_in[head_id], w_out[head_id], score_vec[head_id], entry[1])[5]
        return lax.map(reward_of, (slab_blocks, poolers))
    rewards = lax.map(forward, head_ids)
    center = lax.optimization_barrier(jnp.mean(rewards, axis=0))
    spread = lax.optimization_barrier(jnp.mean((rewards - center) ** 2, axis=0))
    deviation = jnp.sqrt(spread + SPREAD_FLOOR)
    penalized = center - PENALTY * deviation
    seq_pulls = seq_weight[None] * (1.0 - PENALTY * (rewards - center) / deviation) / head_count

    def backward(running, head_id):
        w_first = w_in[head_id]
        w_second = w_out[head_id]
        vector = score_vec[head_id]

        def per_slab(totals, entry):
            slab_rows, pooler, seq_pull = entry
            gate_in, activated, combined, inverse, scores, unused = slab_forward(slab_rows, w_first, w_second, vector, pooler)
            tok_weight = jnp.dot(pooler, seq_pull, precision=PRECISE)
            slopes = tok_weight[:, None] * (vector[None, :] * inverse[:, None] - (scores * inverse * inverse / feature_count)[:, None] * combined)
            slope_half = slopes.astype(jnp.bfloat16)
            back_raw = jnp.dot(slope_half, w_second.T, preferred_element_type=jnp.float32)
            back_gate = (back_raw * silu_slope(gate_in)).astype(jnp.bfloat16)
            hidden_term = slopes + jnp.dot(back_gate, w_first.T, preferred_element_type=jnp.float32)
            part_first = lax.optimization_barrier(jnp.dot(slab_rows.T, back_gate, preferred_element_type=jnp.float32).astype(jnp.bfloat16))
            part_second = lax.optimization_barrier(jnp.dot(activated.T, slope_half, preferred_element_type=jnp.float32).astype(jnp.bfloat16))
            return ((totals[0] + part_first.astype(jnp.float32), totals[1] + part_second.astype(jnp.float32)), hidden_term)
        initial = (jnp.zeros(w_first.shape, jnp.float32), jnp.zeros(w_second.shape, jnp.float32))
        grads_pair, hidden_terms = lax.scan(per_slab, initial, (slab_blocks, poolers, seq_pulls[head_id]))
        return (running + hidden_terms.reshape(slab_count * row_count, feature_count), grads_pair)
    grad_hidden, grads_all = lax.scan(backward, jnp.zeros((slab_count * row_count, feature_count), jnp.float32), head_ids)
    return (penalized, grad_hidden, grads_all[0], grads_all[1])
```

```python
import functools

import jax
import jax.numpy as jnp
from jax import lax
from jax.experimental import pallas as pl
from jax.experimental.pallas import tpu as pltpu
from jax.sharding import PartitionSpec as P

PENALTY = 0.5
SPREAD_FLOOR = 0.25
EPSILON = 1e-05
MESH = pl.DeviceIdType.MESH
AGAINST = (((1,), (1,)), ((), ()))
ALONG = (((0,), (0,)), ((), ()))
F32 = jnp.float32
BF16 = jnp.bfloat16
LANES = 128
CORES = 2
TILE = 256


def dot(a, b):
    return jnp.dot(a, b, preferred_element_type=F32)


def dot_nt(a, b):
    return lax.dot_general(a, b, AGAINST, preferred_element_type=F32)


def sigmoid(v):
    return 1.0 / (1.0 + jnp.exp(-v))


def trunk_kernel(
    sizes,
    len_ref, off_ref, sw_ref, hid_ref, vec_ref, win_hbm, wout_hbm,
    pen_out, gh_out, h_out, act_out, sh_out, bg_out,
    win, wout, z, h, pool, gp, gs, gr, act, bp, bs, br, xr, cs, cr, ps, sc, pens,
    sf, sh, bk, ks, bg, fs, fr, fo, x2s, x2r, ts, zr,
    local_sem, out_sem, send_sem, z_sem, h_sem, pool_sem, g_sem, b_sem, x_sem, c_sem,
    sc_send, sc_recv, k_sem, f_sem, x2_sem, t_send, t_recv,
):
    dp, members, mp, tokens, chunk, ff, seqs, features = sizes
    nh = mp // CORES
    mloc = members // dp
    half = mloc * mp * chunk // CORES
    d = lax.axis_index("dp")
    m = lax.axis_index("member")
    p = lax.axis_index("mp")
    hi = p // CORES
    lo = p % CORES
    sib = hi * CORES + (1 - lo)

    def device(dd, mm, pp):
        return {"dp": dd, "member": mm, "mp": pp}

    def hsem(q, j, s):
        return h_sem.at[(q * mloc + j) * dp + s]

    sent = []

    def push(src, dst, sem, to):
        copy = pltpu.make_async_remote_copy(
            src_ref=src, dst_ref=dst, send_sem=send_sem.at[len(sent)], recv_sem=sem,
            device_id=to, device_id_type=MESH,
        )
        copy.start()
        sent.append(copy)

    def arrived(ref, sem):
        pltpu.make_async_copy(ref, ref, sem).wait()

    load_in = pltpu.make_async_copy(win_hbm.at[0], win, local_sem.at[0])
    load_out = pltpu.make_async_copy(wout_hbm.at[0], wout, local_sem.at[1])
    load_in.start()
    load_out.start()

    group = [
        (a, b, c)
        for a in range(dp) for b in range(members) for c in range(CORES)
        if (a, b, c) != (0, 0, 0)
    ]

    def relative(a, b, c):
        return (
            lax.rem(d + a, dp), lax.rem(m + b, members), lax.rem(lo + c, CORES)
        )

    others_hi = [lax.rem(hi + r, nh) for r in range(1, nh)]
    others_d = [lax.rem(d + r, dp) for r in range(1, dp)]
    barrier = pltpu.get_barrier_semaphore()
    for a, b, c in group:
        dd, mm, cc = relative(a, b, c)
        pl.semaphore_signal(
            barrier, inc=1, device_id=device(dd, mm, hi * CORES + cc), device_id_type=MESH
        )
    for hh in others_hi:
        pl.semaphore_signal(
            barrier, inc=1, device_id=device(d, m, hh * CORES + lo), device_id_type=MESH
        )
    pl.semaphore_wait(barrier, len(group) + nh - 1)

    pltpu.make_async_copy(hid_ref, z.at[m], z_sem.at[m]).start()
    for r in range(1, members):
        push(hid_ref, z.at[m], z_sem.at[m], device(d, lax.rem(m + r, members), p))

    place = lax.broadcasted_iota(jnp.int32, (1, tokens), 1)
    row = lax.broadcasted_iota(jnp.int32, (8, tokens), 0)
    pooled = jnp.zeros((8, tokens), F32)
    weights = jnp.zeros((8, tokens), F32)
    start = jnp.int32(0)
    for i in range(seqs):
        size = len_ref[0, i]
        target = start + lax.rem(off_ref[0, i], size)
        inside = jnp.where((place >= start) & (place < start + size), 1.0, 0.0)
        value = inside / jnp.full((1, tokens), size, jnp.int32).astype(F32)
        value = value + jnp.where(place == target, 1.0, 0.0)
        pooled = jnp.where(row == i, value, pooled)
        weights = jnp.where(row == i, sw_ref[0, i], weights)
        start = start + size
    pool[d, 0] = pooled
    pool[d, 1] = weights
    for dd in others_d:
        push(pool.at[d], pool.at[d], pool_sem.at[d], device(dd, m, p))

    for dd in others_d:
        for j in range(mloc):
            c = dd * mloc + j
            arrived(z.at[c], z_sem.at[c])
            push(z.at[c], h.at[p, j, d], hsem(p, j, d), device(dd, m, p))
    for j in range(mloc):
        c = d * mloc + j
        arrived(z.at[c], z_sem.at[c])
        for hh in others_hi:
            push(z.at[c], h.at[p, j, d], hsem(p, j, d), device(d, m, hh * CORES + lo))
        push(z.at[c], h.at[p, j, d], hsem(p, j, d), device(d, m, sib))
        pltpu.make_async_copy(z.at[c], h.at[p, j, d], hsem(p, j, d)).start()
    for dd in others_d:
        for j in range(mloc):
            arrived(h.at[p, j, dd], hsem(p, j, dd))
            for hh in others_hi:
                push(h.at[p, j, dd], h.at[p, j, dd], hsem(p, j, dd), device(d, m, hh * CORES + lo))
            push(h.at[p, j, dd], h.at[p, j, dd], hsem(p, j, dd), device(d, m, sib))
    for j in range(mloc):
        arrived(h.at[p, j, d], hsem(p, j, d))

    def gate_rows(q, j):
        return pl.ds(pl.multiple_of((j * mp + q) * chunk, chunk), chunk)

    def gate_add(q, first):
        for c in range(0, ff, TILE):
            total = None
            for j in range(mloc):
                left = h[q, j].reshape(dp * tokens, chunk)
                term = dot(left, win[gate_rows(q, j), c:c + TILE])
                total = term if total is None else total + term
            total = total.reshape(dp, tokens, TILE)
            if not first:
                total = total + gp[:, :, c:c + TILE]
            gp[:, :, c:c + TILE] = total

    def all_here(q):
        for j in range(mloc):
            for s in range(dp):
                arrived(h.at[q, j, s], hsem(q, j, s))

    load_in.wait()
    gate_add(p, True)
    all_here(sib)
    gate_add(sib, False)
    for hh in others_hi:
        q = hh * CORES + lo
        for j in range(mloc):
            for s in range(dp):
                arrived(h.at[q, j, s], hsem(q, j, s))
                push(h.at[q, j, s], h.at[q, j, s], hsem(q, j, s), device(d, m, sib))
        gate_add(q, False)
    for k, hh in enumerate(others_hi):
        q = hh * CORES + (1 - lo)
        all_here(q)
        if k < len(others_hi) - 1:
            gate_add(q, False)
            continue
        for s in range(dp):
            for c in range(0, ff, TILE):
                total = gp[s, :, c:c + TILE]
                for j in range(mloc):
                    total = total + dot(h[q, j, s], win[gate_rows(q, j), c:c + TILE])
                gp[s, :, c:c + TILE] = total
                gs[s, :, c:c + TILE] = total.astype(BF16)
            for slot, dd in enumerate(others_d):
                slot = dp - 2 - slot
                push(gs.at[s], gr.at[s, slot], g_sem.at[s * dp + slot], device(dd, m, p))
    keep_h = pltpu.make_async_copy(h, h_out, out_sem.at[0])
    keep_h.start()

    load_out.wait()
    for s in range(dp):
        for slot in range(dp - 1):
            arrived(gr.at[s, slot], g_sem.at[s * dp + slot])
        for c in range(0, ff, TILE):
            gate = gp[s, :, c:c + TILE]
            for slot in range(dp - 1):
                gate = gate + gr[s, slot, :, c:c + TILE].astype(F32)
            gp[s, :, c:c + TILE] = gate
            act[s, :, c:c + TILE] = (gate * sigmoid(gate)).astype(BF16)
        for c in range(0, half, TILE):
            cols = pl.ds(pl.multiple_of((1 - lo) * half + c, TILE), TILE)
            bs[s, :, c:c + TILE] = dot(act[s], wout[:, cols]).astype(BF16)
        push(bs.at[s], br.at[s], b_sem.at[s], device(d, m, sib))
        for c in range(0, half, TILE):
            cols = pl.ds(pl.multiple_of(lo * half + c, TILE), TILE)
            bp[s, :, c:c + TILE] = dot(act[s], wout[:, cols])
        arrived(br.at[s], b_sem.at[s])
        xr[s, hi] = (bp[s] + br[s].astype(F32)).astype(BF16)
        for hh in others_hi:
            push(xr.at[s, hi], xr.at[s, hi], x_sem.at[s * nh + hi], device(d, m, hh * CORES + lo))
    keep_act = pltpu.make_async_copy(act, act_out, out_sem.at[1])
    keep_act.start()

    lane = lax.broadcasted_iota(jnp.int32, (tokens, LANES), 1)
    for s in range(dp):
        for hh in others_hi:
            arrived(xr.at[s, hh], x_sem.at[s * nh + hh])
        squares = jnp.zeros((tokens, 1), F32)
        along = jnp.zeros((tokens, 1), F32)
        for k in range(half // chunk):
            block = lo * (half // chunk) + k
            c = k * chunk
            branch = xr[s, 0, :, c:c + chunk].astype(F32)
            for hh in range(1, nh):
                branch = branch + xr[s, hh, :, c:c + chunk].astype(F32)
            comb = h[block % mp, block // mp, s].astype(F32) + branch
            bp[s, :, c:c + chunk] = comb
            cs[s, :, c:c + chunk] = comb.astype(BF16)
            cols = pl.ds(pl.multiple_of((d * CORES + lo) * half + c, chunk), chunk)
            squares = squares + jnp.sum(comb * comb, axis=1, keepdims=True)
            along = along + jnp.sum(comb * vec_ref[:, cols], axis=1, keepdims=True)
        both = jnp.where(lane == 0, squares, along)
        ps[s] = jnp.transpose(both)[:8]
        mine = (m * dp + d) * CORES + lo
        pltpu.make_async_copy(ps.at[s], sc.at[s, mine], sc_recv.at[s]).start()
        for a, b, c in group:
            dd, mm, cc = relative(a, b, c)
            pltpu.make_async_remote_copy(
                src_ref=ps.at[s], dst_ref=sc.at[s, mine],
                send_sem=sc_send.at[s], recv_sem=sc_recv.at[s],
                device_id=device(dd, mm, hi * CORES + cc), device_id_type=MESH,
            ).start()
        push(cs.at[s], cr.at[s], c_sem.at[s], device(d, m, sib))

    for dd in others_d:
        arrived(pool.at[dd], pool_sem.at[dd])
    for s in range(dp):
        arrived(sc.at[s], sc_recv.at[s])
        pooled = pool[s, 0]

        def head(mm):
            total = sc[s, mm * dp * CORES]
            for i in range(1, dp * CORES):
                total = total + sc[s, mm * dp * CORES + i]
            inv = lax.rsqrt(total[0:1] / features + EPSILON)
            score = total[1:2] * inv
            return inv, score, jnp.sum(score * pooled, axis=1, keepdims=True)

        rewards = [head(mm)[2] for mm in range(members)]
        center = rewards[0]
        for mm in range(1, members):
            center = center + rewards[mm]
        center = center / members
        spread = (rewards[0] - center) ** 2
        for mm in range(1, members):
            spread = spread + (rewards[mm] - center) ** 2
        deviation = jnp.sqrt(spread / members + SPREAD_FLOOR)
        pens[s] = jnp.broadcast_to(center - PENALTY * deviation, (8, LANES))
        inv, score, reward = head(m)
        pull = pool[s, 1] * (1.0 - PENALTY * (reward - center) / deviation) / members
        weight = jnp.sum(pooled * pull, axis=0, keepdims=True)
        by_vec = weight * inv
        by_comb = weight * (score * inv * inv / features)
        rows = lax.broadcasted_iota(jnp.int32, (LANES, tokens), 0)
        both = jnp.transpose(jnp.where(rows == 0, by_vec, by_comb))
        by_vec, by_comb = both[:, 0:1], both[:, 1:2]
        arrived(cr.at[s], c_sem.at[s])
        for own in (True, False):
            base = lo * half if own else (1 - lo) * half
            for c in range(0, half, TILE):
                comb = bp[s, :, c:c + TILE] if own else cr[s, :, c:c + TILE].astype(F32)
                vec = vec_ref[:, pl.ds(pl.multiple_of(d * CORES * half + base + c, TILE), TILE)]
                slope = by_vec * vec - by_comb * comb
                cols = pl.ds(pl.multiple_of(base + c, TILE), TILE)
                sf[s, :, cols] = slope
                sh[s, :, cols] = slope.astype(BF16)
        for c in range(0, ff, TILE):
            term = dot_nt(sh[s], wout[c:c + TILE, :])
            bk[s, :, c:c + TILE] = term
            ks[s, :, c:c + TILE] = term.astype(BF16)
        for slot, dd in enumerate(others_d):
            slot = dp - 2 - slot
            push(ks.at[s], gr.at[s, slot], k_sem.at[s * dp + slot], device(dd, m, p))
    keep_sh = pltpu.make_async_copy(sh, sh_out, out_sem.at[2])
    keep_sh.start()
    spot = lax.broadcasted_iota(jnp.int32, (8, LANES), 1)
    diag = lax.broadcasted_iota(jnp.int32, (8, LANES), 0) == spot
    flat = jnp.sum(jnp.where(diag, pens[d], 0.0), axis=0, keepdims=True)
    pen_out[...] = flat[:, :seqs]

    for s in range(dp):
        for slot in range(dp - 1):
            arrived(gr.at[s, slot], k_sem.at[s * dp + slot])
        for c in range(0, ff, TILE):
            raw = bk[s, :, c:c + TILE]
            for slot in range(dp - 1):
                raw = raw + gr[s, slot, :, c:c + TILE].astype(F32)
            gate = gp[s, :, c:c + TILE]
            sig = sigmoid(gate)
            bg[s, :, c:c + TILE] = (raw * (sig * (1.0 + gate * (1.0 - sig)))).astype(BF16)

        def hidden_term(hh, j, cc):
            first = (j * mp + hh * CORES + cc) * chunk
            return dot_nt(bg[s], win[pl.ds(pl.multiple_of(first, chunk), chunk), :])

        for hh in range(nh):
            for j in range(mloc):
                fs[s, hh, j] = hidden_term(hh, j, 1 - lo).astype(BF16)
        push(fs.at[s], fr.at[s], f_sem.at[s], device(d, m, sib))
        for hh in range(nh):
            for j in range(mloc):
                fo[s, hh, j] = hidden_term(hh, j, lo)
        arrived(fr.at[s], f_sem.at[s])
        for hh in others_hi:
            x2s[s, hh] = (fo[s, hh] + fr[s, hh].astype(F32)).astype(BF16)
            push(x2s.at[s, hh], x2r.at[s, hi], x2_sem.at[s * nh + hi], device(d, m, hh * CORES + lo))
    keep_bg = pltpu.make_async_copy(bg, bg_out, out_sem.at[3])
    keep_bg.start()

    last = []
    for s in range(dp):
        for hh in others_hi:
            arrived(x2r.at[s, hh], x2_sem.at[s * nh + hh])
        for j in range(mloc):
            total = fo[s, hi, j] + fr[s, hi, j].astype(F32)
            for hh in others_hi:
                total = total + x2r[s, hh, j].astype(F32)
            cols = pl.ds(pl.multiple_of((j * mp + p) * chunk, chunk), chunk)
            ts[s, j] = (total + sf[s, :, cols]).astype(BF16)
            to = d * mloc + j
            here = jnp.logical_and(d == s, to == m)
            away = pltpu.make_async_remote_copy(
                src_ref=ts.at[s, j], dst_ref=zr.at[m],
                send_sem=t_send.at[s * mloc + j], recv_sem=t_recv.at[m],
                device_id=device(jnp.int32(s), to, p), device_id_type=MESH,
            )
            near = pltpu.make_async_copy(ts.at[s, j], zr.at[m], t_recv.at[m])

            @pl.when(here)
            def _(near=near):
                near.start()

            @pl.when(jnp.logical_not(here))
            def _(away=away):
                away.start()

            last.append((here, away))

    arrived(zr.at[0], t_recv.at[0])
    total = zr[0].astype(F32)
    for mm in range(1, members):
        arrived(zr.at[mm], t_recv.at[mm])
        total = total + zr[mm].astype(F32)
    gh_out[...] = total

    for copy in sent:
        copy.wait_send()
    for here, away in last:
        @pl.when(jnp.logical_not(here))
        def _(away=away):
            away.wait_send()
    for s in range(dp):
        some = sc.at[s, pl.ds(0, len(group))]
        pltpu.make_async_copy(some, some, sc_send.at[s]).wait()
    for copy in (keep_h, keep_act, keep_sh, keep_bg):
        copy.wait()


def weight_kernel(slabs, h_ref, bg_ref, act_ref, sh_ref, gin_ref, gout_ref):
    def terms(left, right):
        total = None
        for s in range(slabs):
            term = lax.dot_general(left(s), right[s], ALONG, preferred_element_type=F32)
            term = term.astype(BF16).astype(F32)
            total = term if total is None else total + term
        return total

    gin_ref[0] = terms(lambda s: h_ref[0, 0, s], bg_ref)
    gout_ref[0] = terms(lambda s: act_ref[s], sh_ref)


def solution(mesh):
    dp, members, mp = mesh.shape["dp"], mesh.shape["member"], mesh.shape["mp"]

    def local(hidden, w_in, w_out, score_vec, lengths, reward_offset, seq_weight):
        tokens, chunk = hidden.shape
        _, rows, ff = w_in.shape
        seqs = lengths.shape[1]
        features = score_vec.shape[1]
        nh = mp // CORES
        mloc = members // dp
        half = rows // CORES
        peers = dp * members * CORES
        sizes = (dp, members, mp, tokens, chunk, ff, seqs, features)
        smem = pl.BlockSpec(memory_space=pltpu.SMEM)
        vmem = pl.BlockSpec(memory_space=pltpu.VMEM)
        hbm = pl.BlockSpec(memory_space=pl.ANY)
        V = pltpu.VMEM
        dma = lambda n: pltpu.SemaphoreType.DMA((n,))
        sds = jax.ShapeDtypeStruct
        flops = 8 * dp * tokens * rows * ff
        pen, gh, h, act, sh, bg = pl.pallas_call(
            functools.partial(trunk_kernel, sizes),
            out_shape=(
                sds((1, seqs), F32),
                sds((tokens, chunk), F32),
                sds((mp, mloc, dp, tokens, chunk), BF16),
                sds((dp, tokens, ff), BF16),
                sds((dp, tokens, rows), BF16),
                sds((dp, tokens, ff), BF16),
            ),
            in_specs=[smem, smem, smem, hbm, vmem, hbm, hbm],
            out_specs=(vmem, vmem, hbm, hbm, hbm, hbm),
            scratch_shapes=[
                V((rows, ff), BF16),
                V((ff, rows), BF16),
                V((members, tokens, chunk), BF16),
                V((mp, mloc, dp, tokens, chunk), BF16),
                V((dp, 2, 8, tokens), F32),
                V((dp, tokens, ff), F32),
                V((dp, tokens, ff), BF16),
                V((dp, dp - 1, tokens, ff), BF16),
                V((dp, tokens, ff), BF16),
                V((dp, tokens, half), F32),
                V((dp, tokens, half), BF16),
                V((dp, tokens, half), BF16),
                V((dp, nh, tokens, half), BF16),
                V((dp, tokens, half), BF16),
                V((dp, tokens, half), BF16),
                V((dp, 8, tokens), F32),
                V((dp, peers, 8, tokens), F32),
                V((dp, 8, LANES), F32),
                V((dp, tokens, rows), F32),
                V((dp, tokens, rows), BF16),
                V((dp, tokens, ff), F32),
                V((dp, tokens, ff), BF16),
                V((dp, tokens, ff), BF16),
                V((dp, nh, mloc, tokens, chunk), BF16),
                V((dp, nh, mloc, tokens, chunk), BF16),
                V((dp, nh, mloc, tokens, chunk), F32),
                V((dp, nh, mloc, tokens, chunk), BF16),
                V((dp, nh, mloc, tokens, chunk), BF16),
                V((dp, mloc, tokens, chunk), BF16),
                V((members, tokens, chunk), BF16),
                dma(2), dma(4), dma(128), dma(members), dma(mp * mloc * dp), dma(dp),
                dma(dp * dp), dma(dp), dma(dp * nh), dma(dp), dma(dp), dma(dp),
                dma(dp * dp), dma(dp), dma(dp * nh), dma(dp * mloc), dma(members),
            ],
            compiler_params=pltpu.CompilerParams(
                collective_id=0, has_side_effects=True, vmem_limit_bytes=60 * 2**20
            ),
            cost_estimate=pl.CostEstimate(
                flops=flops, bytes_accessed=4 * rows * ff, transcendentals=0
            ),
        )(lengths, reward_offset, seq_weight, hidden, score_vec, w_in, w_out)

        steps = mloc * mp
        out_rows = ff // steps
        whole = lambda *shape: pl.BlockSpec(shape, lambda i: (0,) * len(shape))
        gin, gout = pl.pallas_call(
            functools.partial(weight_kernel, dp),
            grid=(steps,),
            out_shape=(sds((1, rows, ff), F32), sds((1, ff, rows), F32)),
            in_specs=[
                pl.BlockSpec((1, 1, dp, tokens, chunk), lambda i: (i % mp, i // mp, 0, 0, 0)),
                whole(dp, tokens, ff),
                pl.BlockSpec((dp, tokens, out_rows), lambda i: (0, 0, i)),
                whole(dp, tokens, rows),
            ],
            out_specs=(
                pl.BlockSpec((1, chunk, ff), lambda i: (0, i, 0)),
                pl.BlockSpec((1, out_rows, rows), lambda i: (0, i, 0)),
            ),
            compiler_params=pltpu.CompilerParams(vmem_limit_bytes=40 * 2**20),
            cost_estimate=pl.CostEstimate(
                flops=flops // 2, bytes_accessed=8 * rows * ff, transcendentals=0
            ),
        )(h, bg, act, sh)
        return pen, gh, gin, gout

    in_specs = (
        P("dp", ("member", "mp")),
        P("member", "dp", "mp"),
        P("member", "mp", "dp"),
        P("member", None),
        P("dp", None),
        P("dp", None),
        P("dp", None),
    )
    out_specs = (
        P("dp", None),
        P("dp", ("member", "mp")),
        P("member", "dp", "mp"),
        P("member", "mp", "dp"),
    )
    return jax.shard_map(local, mesh=mesh, in_specs=in_specs, out_specs=out_specs, check_vma=False)
```

```python
import functools

import jax
import jax.numpy as jnp
from jax import lax
from jax.experimental import pallas as pl
from jax.experimental.pallas import tpu as pltpu
from jax.sharding import PartitionSpec as P

PENALTY = 0.5
SPREAD_FLOOR = 0.25
EPSILON = 1e-05
MESH = pl.DeviceIdType.MESH
AGAINST = (((1,), (1,)), ((), ()))
ALONG = (((0,), (0,)), ((), ()))
F32 = jnp.float32
BF16 = jnp.bfloat16
LANES = 128
CORES = 2
TILE = 256


def dot(a, b):
    return jnp.dot(a, b, preferred_element_type=F32)


def dot_nt(a, b):
    return lax.dot_general(a, b, AGAINST, preferred_element_type=F32)


def sigmoid(v):
    return 1.0 / (1.0 + jnp.exp(-v))


def trunk_kernel(
    sizes,
    len_ref, off_ref, sw_ref, hid_ref, vec_ref, win_hbm, wout_hbm,
    *rest,
):
    members = sizes[1]
    pen_out, h_out, act_out, sh_out, bg_out = rest[:5]
    chunk_outs = rest[5:5 + members]
    trunk_body(
        sizes, len_ref, off_ref, sw_ref, hid_ref, vec_ref, win_hbm, wout_hbm,
        pen_out, h_out, act_out, sh_out, bg_out, chunk_outs, *rest[5 + members:]
    )


def trunk_body(
    sizes,
    len_ref, off_ref, sw_ref, hid_ref, vec_ref, win_hbm, wout_hbm,
    pen_out, h_out, act_out, sh_out, bg_out, chunk_outs,
    win, wout, z, h, pool, gp, gs, gr, act, bp, bs, br, xr, cs, cr, ps, sc, pens,
    sf, sh, bk, ks, bg, fs, fr, fo, x2s, x2r,
    local_sem, out_sem, send_sem, z_sem, h_sem, pool_sem, g_sem, b_sem, x_sem, c_sem,
    sc_send, sc_recv, k_sem, f_sem, x2_sem,
):
    dp, members, mp, tokens, chunk, ff, seqs, features = sizes
    nh = mp // CORES
    mloc = members // dp
    half = mloc * mp * chunk // CORES
    d = lax.axis_index("dp")
    m = lax.axis_index("member")
    p = lax.axis_index("mp")
    hi = p // CORES
    lo = p % CORES
    sib = hi * CORES + (1 - lo)

    def device(dd, mm, pp):
        return {"dp": dd, "member": mm, "mp": pp}

    def hsem(q, j, s):
        return h_sem.at[(q * mloc + j) * dp + s]

    sent = []

    def push(src, dst, sem, to):
        copy = pltpu.make_async_remote_copy(
            src_ref=src, dst_ref=dst, send_sem=send_sem.at[len(sent)], recv_sem=sem,
            device_id=to, device_id_type=MESH,
        )
        copy.start()
        sent.append(copy)
        return copy

    def arrived(ref, sem):
        pltpu.make_async_copy(ref, ref, sem).wait()

    load_in = pltpu.make_async_copy(win_hbm.at[0], win, local_sem.at[0])
    load_out = pltpu.make_async_copy(wout_hbm.at[0], wout, local_sem.at[1])
    load_in.start()
    load_out.start()

    group = [
        (a, b, c)
        for a in range(dp) for b in range(members) for c in range(CORES)
        if (a, b, c) != (0, 0, 0)
    ]

    def relative(a, b, c):
        return (
            lax.rem(d + a, dp), lax.rem(m + b, members), lax.rem(lo + c, CORES)
        )

    others_hi = [lax.rem(hi + r, nh) for r in range(1, nh)]
    others_d = [lax.rem(d + r, dp) for r in range(1, dp)]
    barrier = pltpu.get_barrier_semaphore()
    for a, b, c in group:
        dd, mm, cc = relative(a, b, c)
        pl.semaphore_signal(
            barrier, inc=1, device_id=device(dd, mm, hi * CORES + cc), device_id_type=MESH
        )
    for hh in others_hi:
        pl.semaphore_signal(
            barrier, inc=1, device_id=device(d, m, hh * CORES + lo), device_id_type=MESH
        )
    pl.semaphore_wait(barrier, len(group) + nh - 1)

    pltpu.make_async_copy(hid_ref, z.at[m], z_sem.at[m]).start()
    for r in range(1, members):
        push(hid_ref, z.at[m], z_sem.at[m], device(d, lax.rem(m + r, members), p))

    place = lax.broadcasted_iota(jnp.int32, (1, tokens), 1)
    row = lax.broadcasted_iota(jnp.int32, (8, tokens), 0)
    pooled = jnp.zeros((8, tokens), F32)
    weights = jnp.zeros((8, tokens), F32)
    start = jnp.int32(0)
    for i in range(seqs):
        size = len_ref[0, i]
        target = start + lax.rem(off_ref[0, i], size)
        inside = jnp.where((place >= start) & (place < start + size), 1.0, 0.0)
        value = inside / jnp.full((1, tokens), size, jnp.int32).astype(F32)
        value = value + jnp.where(place == target, 1.0, 0.0)
        pooled = jnp.where(row == i, value, pooled)
        weights = jnp.where(row == i, sw_ref[0, i], weights)
        start = start + size
    pool[d, 0] = pooled
    pool[d, 1] = weights
    for dd in others_d:
        push(pool.at[d], pool.at[d], pool_sem.at[d], device(dd, m, p))

    for dd in others_d:
        for j in range(mloc):
            c = dd * mloc + j
            arrived(z.at[c], z_sem.at[c])
            push(z.at[c], h.at[p, j, d], hsem(p, j, d), device(dd, m, p))
    for j in range(mloc):
        c = d * mloc + j
        arrived(z.at[c], z_sem.at[c])
        for hh in others_hi:
            push(z.at[c], h.at[p, j, d], hsem(p, j, d), device(d, m, hh * CORES + lo))
        push(z.at[c], h.at[p, j, d], hsem(p, j, d), device(d, m, sib))
        pltpu.make_async_copy(z.at[c], h.at[p, j, d], hsem(p, j, d)).start()
    for dd in others_d:
        for j in range(mloc):
            arrived(h.at[p, j, dd], hsem(p, j, dd))
            for hh in others_hi:
                push(h.at[p, j, dd], h.at[p, j, dd], hsem(p, j, dd), device(d, m, hh * CORES + lo))
            push(h.at[p, j, dd], h.at[p, j, dd], hsem(p, j, dd), device(d, m, sib))
    for j in range(mloc):
        arrived(h.at[p, j, d], hsem(p, j, d))

    def gate_rows(q, j):
        return pl.ds(pl.multiple_of((j * mp + q) * chunk, chunk), chunk)

    def gate_add(q, first):
        for c in range(0, ff, TILE):
            total = None
            for j in range(mloc):
                left = h[q, j].reshape(dp * tokens, chunk)
                term = dot(left, win[gate_rows(q, j), c:c + TILE])
                total = term if total is None else total + term
            total = total.reshape(dp, tokens, TILE)
            if not first:
                total = total + gp[:, :, c:c + TILE]
            gp[:, :, c:c + TILE] = total

    def all_here(q):
        for j in range(mloc):
            for s in range(dp):
                arrived(h.at[q, j, s], hsem(q, j, s))

    waited = []
    tiles = ff // TILE

    def tile_sem(sem, s, slot, t):
        return sem.at[(s * dp + slot) * tiles + t]

    def send_tile(src, s, t, sem):
        copies = []
        for k, dd in enumerate(others_d):
            slot = dp - 2 - k
            copies.append(push(
                src.at[s, t], gr.at[s, slot, t], tile_sem(sem, s, slot, t), device(dd, m, p)
            ))
        return copies

    load_in.wait()
    gate_add(p, True)
    all_here(sib)
    gate_add(sib, False)
    for hh in others_hi:
        q = hh * CORES + lo
        for j in range(mloc):
            for s in range(dp):
                arrived(h.at[q, j, s], hsem(q, j, s))
                push(h.at[q, j, s], h.at[q, j, s], hsem(q, j, s), device(d, m, sib))
        gate_add(q, False)
    for k, hh in enumerate(others_hi):
        q = hh * CORES + (1 - lo)
        all_here(q)
        if k < len(others_hi) - 1:
            gate_add(q, False)
            continue
        early = {}
        for s in range(dp):
            for t in range(ff // TILE):
                cols = slice(t * TILE, (t + 1) * TILE)
                total = gp[s, :, cols]
                for j in range(mloc):
                    total = total + dot(h[q, j, s], win[gate_rows(q, j), cols])
                gp[s, :, cols] = total
                gs[s, t] = total.astype(BF16)
                for copy in early.pop((s - 1, t), ()):
                    copy.wait_send()
                    waited.append(copy)
                early[s, t] = send_tile(gs, s, t, g_sem)
    keep_h = pltpu.make_async_copy(h, h_out, out_sem.at[0])
    keep_h.start()

    load_out.wait()
    halves = half // TILE
    for s in range(dp):
        for t in range(tiles):
            cols = slice(t * TILE, (t + 1) * TILE)
            gate = gp[s, :, cols]
            for slot in range(dp - 1):
                arrived(gr.at[s, slot, t], tile_sem(g_sem, s, slot, t))
                gate = gate + gr[s, slot, t].astype(F32)
            gp[s, :, cols] = gate
            act[s, :, cols] = (gate * sigmoid(gate)).astype(BF16)
        for t in range(halves):
            cols = pl.ds(pl.multiple_of((1 - lo) * half + t * TILE, TILE), TILE)
            bs[s, t] = dot(act[s], wout[:, cols]).astype(BF16)
            push(bs.at[s, t], br.at[s, t], b_sem.at[s * halves + t], device(d, m, sib))
        for t in range(halves):
            cols = pl.ds(pl.multiple_of(lo * half + t * TILE, TILE), TILE)
            term = dot(act[s], wout[:, cols])
            arrived(br.at[s, t], b_sem.at[s * halves + t])
            xr[s, hi, t] = (term + br[s, t].astype(F32)).astype(BF16)
            for hh in others_hi:
                push(
                    xr.at[s, hi, t], xr.at[s, hi, t], x_sem.at[(s * nh + hi) * halves + t],
                    device(d, m, hh * CORES + lo),
                )
    keep_act = pltpu.make_async_copy(act, act_out, out_sem.at[1])
    keep_act.start()

    lane = lax.broadcasted_iota(jnp.int32, (tokens, LANES), 1)

    def combine(s):
        squares = jnp.zeros((tokens, 1), F32)
        along = jnp.zeros((tokens, 1), F32)
        per = TILE // chunk
        for k in range(half // chunk):
            block = lo * (half // chunk) + k
            c = k * chunk
            t, inner = k // per, slice(k % per * chunk, (k % per + 1) * chunk)
            if k % per == 0:
                for hh in others_hi:
                    arrived(xr.at[s, hh, t], x_sem.at[(s * nh + hh) * halves + t])
            branch = xr[s, 0, t, :, inner].astype(F32)
            for hh in range(1, nh):
                branch = branch + xr[s, hh, t, :, inner].astype(F32)
            comb = h[block % mp, block // mp, s].astype(F32) + branch
            bp[s, :, c:c + chunk] = comb
            cs[s, :, c:c + chunk] = comb.astype(BF16)
            cols = pl.ds(pl.multiple_of((d * CORES + lo) * half + c, chunk), chunk)
            squares = squares + jnp.sum(comb * comb, axis=1, keepdims=True)
            along = along + jnp.sum(comb * vec_ref[:, cols], axis=1, keepdims=True)
        both = jnp.where(lane == 0, squares, along)
        ps[s] = jnp.transpose(both)[:8]
        mine = (m * dp + d) * CORES + lo
        pltpu.make_async_copy(ps.at[s], sc.at[s, mine], sc_recv.at[s]).start()
        for a, b, c in group:
            dd, mm, cc = relative(a, b, c)
            pltpu.make_async_remote_copy(
                src_ref=ps.at[s], dst_ref=sc.at[s, mine],
                send_sem=sc_send.at[s], recv_sem=sc_recv.at[s],
                device_id=device(dd, mm, hi * CORES + cc), device_id_type=MESH,
            ).start()
        push(cs.at[s], cr.at[s], c_sem.at[s], device(d, m, sib))

    def slopes_of(s):
        arrived(sc.at[s], sc_recv.at[s])
        pooled = pool[s, 0]

        def head(mm):
            total = sc[s, mm * dp * CORES]
            for i in range(1, dp * CORES):
                total = total + sc[s, mm * dp * CORES + i]
            inv = lax.rsqrt(total[0:1] / features + EPSILON)
            score = total[1:2] * inv
            return inv, score, jnp.sum(score * pooled, axis=1, keepdims=True)

        rewards = [head(mm)[2] for mm in range(members)]
        center = rewards[0]
        for mm in range(1, members):
            center = center + rewards[mm]
        center = center / members
        spread = (rewards[0] - center) ** 2
        for mm in range(1, members):
            spread = spread + (rewards[mm] - center) ** 2
        deviation = jnp.sqrt(spread / members + SPREAD_FLOOR)
        pens[s] = jnp.broadcast_to(center - PENALTY * deviation, (8, LANES))
        inv, score, reward = head(m)
        pull = pool[s, 1] * (1.0 - PENALTY * (reward - center) / deviation) / members
        weight = jnp.sum(pooled * pull, axis=0, keepdims=True)
        by_vec = weight * inv
        by_comb = weight * (score * inv * inv / features)
        rows = lax.broadcasted_iota(jnp.int32, (LANES, tokens), 0)
        both = jnp.transpose(jnp.where(rows == 0, by_vec, by_comb))
        by_vec, by_comb = both[:, 0:1], both[:, 1:2]
        arrived(cr.at[s], c_sem.at[s])
        for own in (True, False):
            base = lo * half if own else (1 - lo) * half
            for c in range(0, half, TILE):
                comb = bp[s, :, c:c + TILE] if own else cr[s, :, c:c + TILE].astype(F32)
                vec = vec_ref[:, pl.ds(pl.multiple_of(d * CORES * half + base + c, TILE), TILE)]
                slope = by_vec * vec - by_comb * comb
                cols = pl.ds(pl.multiple_of(base + c, TILE), TILE)
                sf[s, :, cols] = slope
                sh[s, :, cols] = slope.astype(BF16)
        for t in range(tiles):
            cols = slice(t * TILE, (t + 1) * TILE)
            term = dot_nt(sh[s], wout[cols, :])
            bk[s, :, cols] = term
            ks[s, t] = term.astype(BF16)
            send_tile(ks, s, t, k_sem)

    for dd in others_d:
        arrived(pool.at[dd], pool_sem.at[dd])
    for s in range(dp):
        combine(s)
        slopes_of(s)
    keep_sh = pltpu.make_async_copy(sh, sh_out, out_sem.at[2])
    keep_sh.start()
    spot = lax.broadcasted_iota(jnp.int32, (8, LANES), 1)
    diag = lax.broadcasted_iota(jnp.int32, (8, LANES), 0) == spot
    flat = jnp.sum(jnp.where(diag, pens[d], 0.0), axis=0, keepdims=True)
    pen_out[...] = flat[:, :seqs]

    for s in range(dp):
        for t in range(tiles):
            cols = slice(t * TILE, (t + 1) * TILE)
            raw = bk[s, :, cols]
            for slot in range(dp - 1):
                arrived(gr.at[s, slot, t], tile_sem(k_sem, s, slot, t))
                raw = raw + gr[s, slot, t].astype(F32)
            gate = gp[s, :, cols]
            sig = sigmoid(gate)
            bg[s, :, cols] = (raw * (sig * (1.0 + gate * (1.0 - sig)))).astype(BF16)

        def hidden_term(hh, j, cc):
            first = (j * mp + hh * CORES + cc) * chunk
            return dot_nt(bg[s], win[pl.ds(pl.multiple_of(first, chunk), chunk), :])

        for hh in others_hi + [hi]:
            for j in range(mloc):
                fs[s, hh, j] = hidden_term(hh, j, 1 - lo).astype(BF16)
            push(fs.at[s, hh], fr.at[s, hh], f_sem.at[s * nh + hh], device(d, m, sib))
            for j in range(mloc):
                fo[s, hh, j] = hidden_term(hh, j, lo)
            if hh is hi:
                continue
            arrived(fr.at[s, hh], f_sem.at[s * nh + hh])
            x2s[s, hh] = (fo[s, hh] + fr[s, hh].astype(F32)).astype(BF16)
            push(x2s.at[s, hh], x2r.at[s, hi], x2_sem.at[s * nh + hi], device(d, m, hh * CORES + lo))
    keep_bg = pltpu.make_async_copy(bg, bg_out, out_sem.at[3])
    keep_bg.start()

    for s in range(dp):
        arrived(fr.at[s, hi], f_sem.at[s * nh + hi])
        for hh in others_hi:
            arrived(x2r.at[s, hh], x2_sem.at[s * nh + hh])
    for k, out in enumerate(chunk_outs):
        n = lax.rem(m + k, members)
        s, j = n // mloc, lax.rem(n, mloc)
        total = fo[s, hi, j] + fr[s, hi, j].astype(F32)
        for hh in others_hi:
            total = total + x2r[s, hh, j].astype(F32)
        cols = pl.ds(pl.multiple_of((j * mp + p) * chunk, chunk), chunk)
        out[...] = (total + sf[s, :, cols]).astype(BF16)

    for copy in sent:
        if all(copy is not done for done in waited):
            copy.wait_send()
    for s in range(dp):
        some = sc.at[s, pl.ds(0, len(group))]
        pltpu.make_async_copy(some, some, sc_send.at[s]).wait()
    for copy in (keep_h, keep_act, keep_sh, keep_bg):
        copy.wait()


def weight_kernel(slabs, h_ref, bg_ref, act_ref, sh_ref, pen_ref, gin_ref, gout_ref, pen_out):
    def terms(left, right):
        total = None
        for s in range(slabs):
            term = lax.dot_general(left(s), right[s], ALONG, preferred_element_type=F32)
            term = term.astype(BF16).astype(F32)
            total = term if total is None else total + term
        return total

    pen_out[...] = pen_ref[...]
    gin_ref[0] = terms(lambda s: h_ref[0, 0, s], bg_ref)
    gout_ref[0] = terms(lambda s: act_ref[s], sh_ref)


def solution(mesh):
    dp, members, mp = mesh.shape["dp"], mesh.shape["member"], mesh.shape["mp"]

    def local(hidden, w_in, w_out, score_vec, lengths, reward_offset, seq_weight):
        tokens, chunk = hidden.shape
        _, rows, ff = w_in.shape
        seqs = lengths.shape[1]
        features = score_vec.shape[1]
        nh = mp // CORES
        mloc = members // dp
        half = rows // CORES
        peers = dp * members * CORES
        sizes = (dp, members, mp, tokens, chunk, ff, seqs, features)
        smem = pl.BlockSpec(memory_space=pltpu.SMEM)
        vmem = pl.BlockSpec(memory_space=pltpu.VMEM)
        hbm = pl.BlockSpec(memory_space=pl.ANY)
        V = pltpu.VMEM
        dma = lambda n: pltpu.SemaphoreType.DMA((n,))
        sds = jax.ShapeDtypeStruct
        sends = 64 + 16 * dp + 2 * dp * dp * (ff // TILE)
        flops = 8 * dp * tokens * rows * ff
        pen, h, act, sh, bg, *chunks = pl.pallas_call(
            functools.partial(trunk_kernel, sizes),
            out_shape=(
                sds((1, seqs), F32),
                sds((mp, mloc, dp, tokens, chunk), BF16),
                sds((dp, tokens, ff), BF16),
                sds((dp, tokens, rows), BF16),
                sds((dp, tokens, ff), BF16),
            ) + (sds((tokens, chunk), BF16),) * members,
            in_specs=[smem, smem, smem, hbm, vmem, hbm, hbm],
            out_specs=(vmem, hbm, hbm, hbm, hbm) + (vmem,) * members,
            scratch_shapes=[
                V((rows, ff), BF16),
                V((ff, rows), BF16),
                V((members, tokens, chunk), BF16),
                V((mp, mloc, dp, tokens, chunk), BF16),
                V((dp, 2, 8, tokens), F32),
                V((dp, tokens, ff), F32),
                V((dp, ff // TILE, tokens, TILE), BF16),
                V((dp, dp - 1, ff // TILE, tokens, TILE), BF16),
                V((dp, tokens, ff), BF16),
                V((dp, tokens, half), F32),
                V((dp, half // TILE, tokens, TILE), BF16),
                V((dp, half // TILE, tokens, TILE), BF16),
                V((dp, nh, half // TILE, tokens, TILE), BF16),
                V((dp, tokens, half), BF16),
                V((dp, tokens, half), BF16),
                V((dp, 8, tokens), F32),
                V((dp, peers, 8, tokens), F32),
                V((dp, 8, LANES), F32),
                V((dp, tokens, rows), F32),
                V((dp, tokens, rows), BF16),
                V((dp, tokens, ff), F32),
                V((dp, ff // TILE, tokens, TILE), BF16),
                V((dp, tokens, ff), BF16),
                V((dp, nh, mloc, tokens, chunk), BF16),
                V((dp, nh, mloc, tokens, chunk), BF16),
                V((dp, nh, mloc, tokens, chunk), F32),
                V((dp, nh, mloc, tokens, chunk), BF16),
                V((dp, nh, mloc, tokens, chunk), BF16),
                dma(2), dma(4), dma(sends), dma(members), dma(mp * mloc * dp), dma(dp),
                dma(dp * dp * (ff // TILE)), dma(dp * (half // TILE)),
                dma(dp * nh * (half // TILE)), dma(dp), dma(dp), dma(dp),
                dma(dp * dp * (ff // TILE)), dma(dp * nh), dma(dp * nh),
            ],
            compiler_params=pltpu.CompilerParams(
                collective_id=0, has_side_effects=True, vmem_limit_bytes=60 * 2**20
            ),
            cost_estimate=pl.CostEstimate(
                flops=flops, bytes_accessed=4 * rows * ff, transcendentals=0
            ),
        )(lengths, reward_offset, seq_weight, hidden, score_vec, w_in, w_out)

        steps = mloc * mp
        out_rows = ff // steps
        whole = lambda *shape: pl.BlockSpec(shape, lambda i: (0,) * len(shape))
        moved = []
        for k in range(members):
            pairs = []
            for dd in range(dp):
                for mm in range(members):
                    n = (k + mm) % members
                    to = (n // mloc) * members + dd * mloc + n % mloc
                    pairs.append((dd * members + mm, to))
            moved.append(lax.ppermute(chunks[k], ("dp", "member"), pairs))
        gin, gout, pen = pl.pallas_call(
            functools.partial(weight_kernel, dp),
            grid=(steps,),
            out_shape=(sds((1, rows, ff), F32), sds((1, ff, rows), F32), sds((1, seqs), F32)),
            in_specs=[
                pl.BlockSpec((1, 1, dp, tokens, chunk), lambda i: (i % mp, i // mp, 0, 0, 0)),
                whole(dp, tokens, ff),
                pl.BlockSpec((dp, tokens, out_rows), lambda i: (0, 0, i)),
                whole(dp, tokens, rows),
                whole(1, seqs),
            ],
            out_specs=(
                pl.BlockSpec((1, chunk, ff), lambda i: (0, i, 0)),
                pl.BlockSpec((1, out_rows, rows), lambda i: (0, i, 0)),
                whole(1, seqs),
            ),
            compiler_params=pltpu.CompilerParams(vmem_limit_bytes=60 * 2**20),
            cost_estimate=pl.CostEstimate(
                flops=flops // 2, bytes_accessed=8 * rows * ff, transcendentals=0
            ),
        )(h, bg, act, sh, pen)
        gh = moved[0].astype(F32)
        for part in moved[1:]:
            gh = gh + part.astype(F32)
        return pen, gh, gin, gout

    in_specs = (
        P("dp", ("member", "mp")),
        P("member", "dp", "mp"),
        P("member", "mp", "dp"),
        P("member", None),
        P("dp", None),
        P("dp", None),
        P("dp", None),
    )
    out_specs = (
        P("dp", None),
        P("dp", ("member", "mp")),
        P("member", "dp", "mp"),
        P("member", "mp", "dp"),
    )
    return jax.shard_map(local, mesh=mesh, in_specs=in_specs, out_specs=out_specs, check_vma=False)
```

```python
import functools

import jax
import jax.numpy as jnp
from jax import lax
from jax.experimental import pallas as pl
from jax.experimental.pallas import tpu as pltpu
from jax.sharding import PartitionSpec as P

PENALTY = 0.5
SPREAD_FLOOR = 0.25
EPSILON = 1e-05
MESH = pl.DeviceIdType.MESH
AGAINST = (((1,), (1,)), ((), ()))
ALONG = (((0,), (0,)), ((), ()))
F32 = jnp.float32
BF16 = jnp.bfloat16
LANES = 128
CORES = 2
TILE = 256


def dot(a, b):
    return jnp.dot(a, b, preferred_element_type=F32)


def dot_nt(a, b):
    return lax.dot_general(a, b, AGAINST, preferred_element_type=F32)


def sigmoid(v):
    return 1.0 / (1.0 + jnp.exp(-v))


def trunk_kernel(
    sizes,
    len_ref, off_ref, sw_ref, hid_ref, vec_ref, win_hbm, wout_hbm,
    pen_out, gh_out, h_out, act_out, sh_out, bg_out,
    win, wout, z, h, pool, gp, gs, gr, act, bp, bs, br, xr, cs, cr, ps, sc, pens,
    sf, sh, bk, ks, bg, fs, fr, fo, x2s, x2r, ts, zr,
    local_sem, out_sem, send_sem, z_sem, h_sem, pool_sem, g_sem, b_sem, x_sem, c_sem,
    sc_send, sc_recv, k_sem, f_sem, x2_sem, t_send, t_recv,
):
    dp, members, mp, tokens, chunk, ff, seqs, features = sizes
    nh = mp // CORES
    mloc = members // dp
    half = mloc * mp * chunk // CORES
    d = lax.axis_index("dp")
    m = lax.axis_index("member")
    p = lax.axis_index("mp")
    hi = p // CORES
    lo = p % CORES
    sib = hi * CORES + (1 - lo)

    def device(dd, mm, pp):
        return {"dp": dd, "member": mm, "mp": pp}

    def hsem(q, j, s):
        return h_sem.at[(q * mloc + j) * dp + s]

    sent = []

    def push(src, dst, sem, to, now=True):
        copy = pltpu.make_async_remote_copy(
            src_ref=src, dst_ref=dst, send_sem=send_sem.at[len(sent)], recv_sem=sem,
            device_id=to, device_id_type=MESH,
        )
        if now:
            copy.start()
        sent.append(copy)
        return copy

    def arrived(ref, sem):
        pltpu.make_async_copy(ref, ref, sem).wait()

    load_in = pltpu.make_async_copy(win_hbm.at[0], win, local_sem.at[0])
    load_out = pltpu.make_async_copy(wout_hbm.at[0], wout, local_sem.at[1])
    load_in.start()
    load_out.start()

    group = [
        (a, b, c)
        for a in range(dp) for b in range(members) for c in range(CORES)
        if (a, b, c) != (0, 0, 0)
    ]

    def relative(a, b, c):
        return (
            lax.rem(d + a, dp), lax.rem(m + b, members), lax.rem(lo + c, CORES)
        )

    others_hi = [lax.rem(hi + r, nh) for r in range(1, nh)]
    others_d = [lax.rem(d + r, dp) for r in range(1, dp)]
    barrier = pltpu.get_barrier_semaphore()
    for a, b, c in group:
        dd, mm, cc = relative(a, b, c)
        pl.semaphore_signal(
            barrier, inc=1, device_id=device(dd, mm, hi * CORES + cc), device_id_type=MESH
        )
    for hh in others_hi:
        pl.semaphore_signal(
            barrier, inc=1, device_id=device(d, m, hh * CORES + lo), device_id_type=MESH
        )
    pl.semaphore_wait(barrier, len(group) + nh - 1)

    pltpu.make_async_copy(hid_ref, z.at[m], z_sem.at[m]).start()
    for r in range(1, members):
        push(hid_ref, z.at[m], z_sem.at[m], device(d, lax.rem(m + r, members), p))

    place = lax.broadcasted_iota(jnp.int32, (1, tokens), 1)
    row = lax.broadcasted_iota(jnp.int32, (8, tokens), 0)
    pooled = jnp.zeros((8, tokens), F32)
    weights = jnp.zeros((8, tokens), F32)
    start = jnp.int32(0)
    for i in range(seqs):
        size = len_ref[0, i]
        target = start + lax.rem(off_ref[0, i], size)
        inside = jnp.where((place >= start) & (place < start + size), 1.0, 0.0)
        value = inside / jnp.full((1, tokens), size, jnp.int32).astype(F32)
        value = value + jnp.where(place == target, 1.0, 0.0)
        pooled = jnp.where(row == i, value, pooled)
        weights = jnp.where(row == i, sw_ref[0, i], weights)
        start = start + size
    pool[d, 0] = pooled
    pool[d, 1] = weights
    for dd in others_d:
        push(pool.at[d], pool.at[d], pool_sem.at[d], device(dd, m, p))

    across, along_mp = [], []
    for dd in others_d:
        for j in range(mloc):
            c = dd * mloc + j
            across.append((c, [push(
                z.at[c], h.at[p, j, d], hsem(p, j, d), device(dd, m, p), False
            )]))
    for j in range(mloc):
        c = d * mloc + j
        copies = [
            push(z.at[c], h.at[p, j, d], hsem(p, j, d), device(d, m, to), False)
            for to in [hh * CORES + lo for hh in others_hi] + [sib]
        ]
        copies.append(pltpu.make_async_copy(z.at[c], h.at[p, j, d], hsem(p, j, d)))
        along_mp.append((c, copies))

    def forward(entries):
        for c, copies in entries:
            arrived(z.at[c], z_sem.at[c])
            for copy in copies:
                copy.start()

    near_own = m // mloc == d

    @pl.when(near_own)
    def _():
        forward(along_mp + across)

    @pl.when(jnp.logical_not(near_own))
    def _():
        forward(across + along_mp)

    for dd in others_d:
        for j in range(mloc):
            arrived(h.at[p, j, dd], hsem(p, j, dd))
            for hh in others_hi:
                push(h.at[p, j, dd], h.at[p, j, dd], hsem(p, j, dd), device(d, m, hh * CORES + lo))
            push(h.at[p, j, dd], h.at[p, j, dd], hsem(p, j, dd), device(d, m, sib))
    for j in range(mloc):
        arrived(h.at[p, j, d], hsem(p, j, d))

    def gate_rows(q, j):
        return pl.ds(pl.multiple_of((j * mp + q) * chunk, chunk), chunk)

    def gate_add(q, first):
        for c in range(0, ff, TILE):
            total = None
            for j in range(mloc):
                left = h[q, j].reshape(dp * tokens, chunk)
                term = dot(left, win[gate_rows(q, j), c:c + TILE])
                total = term if total is None else total + term
            total = total.reshape(dp, tokens, TILE)
            if not first:
                total = total + gp[:, :, c:c + TILE]
            gp[:, :, c:c + TILE] = total

    def all_here(q):
        for j in range(mloc):
            for s in range(dp):
                arrived(h.at[q, j, s], hsem(q, j, s))

    waited = []
    tiles = ff // TILE

    def tile_sem(sem, s, slot, t):
        return sem.at[(s * dp + slot) * tiles + t]

    def send_tile(src, s, t, sem):
        copies = []
        for k, dd in enumerate(others_d):
            slot = dp - 2 - k
            copies.append(push(
                src.at[s, t], gr.at[s, slot, t], tile_sem(sem, s, slot, t), device(dd, m, p)
            ))
        return copies

    load_in.wait()
    gate_add(p, True)
    all_here(sib)
    gate_add(sib, False)
    for hh in others_hi:
        q = hh * CORES + lo
        for j in range(mloc):
            for s in range(dp):
                arrived(h.at[q, j, s], hsem(q, j, s))
                push(h.at[q, j, s], h.at[q, j, s], hsem(q, j, s), device(d, m, sib))
        gate_add(q, False)
    for k, hh in enumerate(others_hi):
        q = hh * CORES + (1 - lo)
        all_here(q)
        if k < len(others_hi) - 1:
            gate_add(q, False)
            continue
        early = {}
        for s in range(dp):
            for t in range(ff // TILE):
                cols = slice(t * TILE, (t + 1) * TILE)
                total = gp[s, :, cols]
                for j in range(mloc):
                    total = total + dot(h[q, j, s], win[gate_rows(q, j), cols])
                gp[s, :, cols] = total
                gs[s, t] = total.astype(BF16)
                for copy in early.pop((s - 1, t), ()):
                    copy.wait_send()
                    waited.append(copy)
                early[s, t] = send_tile(gs, s, t, g_sem)
    keep_h = pltpu.make_async_copy(h, h_out, out_sem.at[0])
    keep_h.start()

    load_out.wait()
    halves = half // TILE
    for s in range(dp):
        for t in range(tiles):
            cols = slice(t * TILE, (t + 1) * TILE)
            gate = gp[s, :, cols]
            for slot in range(dp - 1):
                arrived(gr.at[s, slot, t], tile_sem(g_sem, s, slot, t))
                gate = gate + gr[s, slot, t].astype(F32)
            gp[s, :, cols] = gate
            act[s, :, cols] = (gate * sigmoid(gate)).astype(BF16)
        for t in range(halves):
            cols = pl.ds(pl.multiple_of((1 - lo) * half + t * TILE, TILE), TILE)
            bs[s, t] = dot(act[s], wout[:, cols]).astype(BF16)
            push(bs.at[s, t], br.at[s, t], b_sem.at[s * halves + t], device(d, m, sib))
        for t in range(halves):
            cols = pl.ds(pl.multiple_of(lo * half + t * TILE, TILE), TILE)
            term = dot(act[s], wout[:, cols])
            arrived(br.at[s, t], b_sem.at[s * halves + t])
            xr[s, hi, t] = (term + br[s, t].astype(F32)).astype(BF16)
            for hh in others_hi:
                push(
                    xr.at[s, hi, t], xr.at[s, hi, t], x_sem.at[(s * nh + hi) * halves + t],
                    device(d, m, hh * CORES + lo),
                )
    keep_act = pltpu.make_async_copy(act, act_out, out_sem.at[1])
    keep_act.start()

    lane = lax.broadcasted_iota(jnp.int32, (tokens, LANES), 1)

    def combine(s):
        squares = jnp.zeros((tokens, 1), F32)
        along = jnp.zeros((tokens, 1), F32)
        per = TILE // chunk
        for k in range(half // chunk):
            block = lo * (half // chunk) + k
            c = k * chunk
            t, inner = k // per, slice(k % per * chunk, (k % per + 1) * chunk)
            if k % per == 0:
                for hh in others_hi:
                    arrived(xr.at[s, hh, t], x_sem.at[(s * nh + hh) * halves + t])
            branch = xr[s, 0, t, :, inner].astype(F32)
            for hh in range(1, nh):
                branch = branch + xr[s, hh, t, :, inner].astype(F32)
            comb = h[block % mp, block // mp, s].astype(F32) + branch
            bp[s, :, c:c + chunk] = comb
            cs[s, :, c:c + chunk] = comb.astype(BF16)
            cols = pl.ds(pl.multiple_of((d * CORES + lo) * half + c, chunk), chunk)
            squares = squares + jnp.sum(comb * comb, axis=1, keepdims=True)
            along = along + jnp.sum(comb * vec_ref[:, cols], axis=1, keepdims=True)
        both = jnp.where(lane == 0, squares, along)
        ps[s] = jnp.transpose(both)[:8]
        mine = (m * dp + d) * CORES + lo
        pltpu.make_async_copy(ps.at[s], sc.at[s, mine], sc_recv.at[s]).start()
        for a, b, c in group:
            dd, mm, cc = relative(a, b, c)
            pltpu.make_async_remote_copy(
                src_ref=ps.at[s], dst_ref=sc.at[s, mine],
                send_sem=sc_send.at[s], recv_sem=sc_recv.at[s],
                device_id=device(dd, mm, hi * CORES + cc), device_id_type=MESH,
            ).start()
        push(cs.at[s], cr.at[s], c_sem.at[s], device(d, m, sib))

    def slopes_of(s):
        arrived(sc.at[s], sc_recv.at[s])
        pooled = pool[s, 0]

        def head(mm):
            total = sc[s, mm * dp * CORES]
            for i in range(1, dp * CORES):
                total = total + sc[s, mm * dp * CORES + i]
            inv = lax.rsqrt(total[0:1] / features + EPSILON)
            score = total[1:2] * inv
            return inv, score, jnp.sum(score * pooled, axis=1, keepdims=True)

        rewards = [head(mm)[2] for mm in range(members)]
        center = rewards[0]
        for mm in range(1, members):
            center = center + rewards[mm]
        center = center / members
        spread = (rewards[0] - center) ** 2
        for mm in range(1, members):
            spread = spread + (rewards[mm] - center) ** 2
        deviation = jnp.sqrt(spread / members + SPREAD_FLOOR)
        pens[s] = jnp.broadcast_to(center - PENALTY * deviation, (8, LANES))
        inv, score, reward = head(m)
        pull = pool[s, 1] * (1.0 - PENALTY * (reward - center) / deviation) / members
        weight = jnp.sum(pooled * pull, axis=0, keepdims=True)
        by_vec = weight * inv
        by_comb = weight * (score * inv * inv / features)
        rows = lax.broadcasted_iota(jnp.int32, (LANES, tokens), 0)
        both = jnp.transpose(jnp.where(rows == 0, by_vec, by_comb))
        by_vec, by_comb = both[:, 0:1], both[:, 1:2]
        arrived(cr.at[s], c_sem.at[s])
        for own in (True, False):
            base = lo * half if own else (1 - lo) * half
            for c in range(0, half, TILE):
                comb = bp[s, :, c:c + TILE] if own else cr[s, :, c:c + TILE].astype(F32)
                vec = vec_ref[:, pl.ds(pl.multiple_of(d * CORES * half + base + c, TILE), TILE)]
                slope = by_vec * vec - by_comb * comb
                cols = pl.ds(pl.multiple_of(base + c, TILE), TILE)
                sf[s, :, cols] = slope
                sh[s, :, cols] = slope.astype(BF16)
        for t in range(tiles):
            cols = slice(t * TILE, (t + 1) * TILE)
            term = dot_nt(sh[s], wout[cols, :])
            bk[s, :, cols] = term
            ks[s, t] = term.astype(BF16)
            send_tile(ks, s, t, k_sem)

    for dd in others_d:
        arrived(pool.at[dd], pool_sem.at[dd])
    for s in range(dp):
        combine(s)
        slopes_of(s)
    keep_sh = pltpu.make_async_copy(sh, sh_out, out_sem.at[2])
    keep_sh.start()
    spot = lax.broadcasted_iota(jnp.int32, (8, LANES), 1)
    diag = lax.broadcasted_iota(jnp.int32, (8, LANES), 0) == spot
    flat = jnp.sum(jnp.where(diag, pens[d], 0.0), axis=0, keepdims=True)
    pen_out[...] = flat[:, :seqs]

    last = []

    def finish(s):
        arrived(fr.at[s, hi], f_sem.at[s * nh + hi])
        for hh in others_hi:
            arrived(x2r.at[s, hh], x2_sem.at[s * nh + hh])
        for j in range(mloc):
            total = fo[s, hi, j] + fr[s, hi, j].astype(F32)
            for hh in others_hi:
                total = total + x2r[s, hh, j].astype(F32)
            cols = pl.ds(pl.multiple_of((j * mp + p) * chunk, chunk), chunk)
            ts[s, j] = (total + sf[s, :, cols]).astype(BF16)
            to = d * mloc + j
            here = jnp.logical_and(d == s, to == m)
            away = pltpu.make_async_remote_copy(
                src_ref=ts.at[s, j], dst_ref=zr.at[m],
                send_sem=t_send.at[s * mloc + j], recv_sem=t_recv.at[m],
                device_id=device(jnp.int32(s), to, p), device_id_type=MESH,
            )
            near = pltpu.make_async_copy(ts.at[s, j], zr.at[m], t_recv.at[m])

            @pl.when(here)
            def _(near=near):
                near.start()

            @pl.when(jnp.logical_not(here))
            def _(away=away):
                away.start()

            last.append((here, away))

    for s in range(dp):
        for t in range(tiles):
            cols = slice(t * TILE, (t + 1) * TILE)
            raw = bk[s, :, cols]
            for slot in range(dp - 1):
                arrived(gr.at[s, slot, t], tile_sem(k_sem, s, slot, t))
                raw = raw + gr[s, slot, t].astype(F32)
            gate = gp[s, :, cols]
            sig = sigmoid(gate)
            bg[s, :, cols] = (raw * (sig * (1.0 + gate * (1.0 - sig)))).astype(BF16)

        def hidden_term(hh, j, cc):
            first = (j * mp + hh * CORES + cc) * chunk
            return dot_nt(bg[s], win[pl.ds(pl.multiple_of(first, chunk), chunk), :])

        for hh in others_hi + [hi]:
            for j in range(mloc):
                fs[s, hh, j] = hidden_term(hh, j, 1 - lo).astype(BF16)
            push(fs.at[s, hh], fr.at[s, hh], f_sem.at[s * nh + hh], device(d, m, sib))
            for j in range(mloc):
                fo[s, hh, j] = hidden_term(hh, j, lo)
            if hh is hi:
                continue
            arrived(fr.at[s, hh], f_sem.at[s * nh + hh])
            x2s[s, hh] = (fo[s, hh] + fr[s, hh].astype(F32)).astype(BF16)
            push(x2s.at[s, hh], x2r.at[s, hi], x2_sem.at[s * nh + hi], device(d, m, hh * CORES + lo))
        if s > 0:
            finish(s - 1)
    keep_bg = pltpu.make_async_copy(bg, bg_out, out_sem.at[3])
    keep_bg.start()
    finish(dp - 1)

    for mm in range(members):
        arrived(zr.at[mm], t_recv.at[mm])
    total = zr[0].astype(F32)
    for mm in range(1, members):
        total = total + zr[mm].astype(F32)
    gh_out[...] = total

    for copy in sent:
        if all(copy is not done for done in waited):
            copy.wait_send()
    for here, away in last:
        @pl.when(jnp.logical_not(here))
        def _(away=away):
            away.wait_send()
    for s in range(dp):
        some = sc.at[s, pl.ds(0, len(group))]
        pltpu.make_async_copy(some, some, sc_send.at[s]).wait()
    for copy in (keep_h, keep_act, keep_sh, keep_bg):
        copy.wait()


def weight_kernel(
    h_ref, bg_ref, act_ref, sh_ref, pen_ref, gh_ref, gin_ref, gout_ref, pen_out, gh_out
):
    pen_out[...] = pen_ref[...]
    gh_out[...] = gh_ref[...]

    def flat(ref):
        value = ref[...]
        return value.reshape(value.shape[-3] * value.shape[-2], value.shape[-1])

    def product(left, right):
        return lax.dot_general(left, right, ALONG, preferred_element_type=F32)

    gin_ref[0] = product(flat(h_ref), flat(bg_ref))
    gout_ref[0] = product(flat(act_ref), flat(sh_ref))


def solution(mesh):
    dp, members, mp = mesh.shape["dp"], mesh.shape["member"], mesh.shape["mp"]

    def local(hidden, w_in, w_out, score_vec, lengths, reward_offset, seq_weight):
        tokens, chunk = hidden.shape
        _, rows, ff = w_in.shape
        seqs = lengths.shape[1]
        features = score_vec.shape[1]
        nh = mp // CORES
        mloc = members // dp
        half = rows // CORES
        peers = dp * members * CORES
        sizes = (dp, members, mp, tokens, chunk, ff, seqs, features)
        smem = pl.BlockSpec(memory_space=pltpu.SMEM)
        vmem = pl.BlockSpec(memory_space=pltpu.VMEM)
        hbm = pl.BlockSpec(memory_space=pl.ANY)
        V = pltpu.VMEM
        dma = lambda n: pltpu.SemaphoreType.DMA((n,))
        sds = jax.ShapeDtypeStruct
        sends = 64 + 16 * dp + 2 * dp * dp * (ff // TILE)
        flops = 8 * dp * tokens * rows * ff
        pen, gh, h, act, sh, bg = pl.pallas_call(
            functools.partial(trunk_kernel, sizes),
            out_shape=(
                sds((1, seqs), F32),
                sds((tokens, chunk), F32),
                sds((mp, mloc, dp, tokens, chunk), BF16),
                sds((dp, tokens, ff), BF16),
                sds((dp, tokens, rows), BF16),
                sds((dp, tokens, ff), BF16),
            ),
            in_specs=[smem, smem, smem, hbm, vmem, hbm, hbm],
            out_specs=(vmem, vmem, hbm, hbm, hbm, hbm),
            scratch_shapes=[
                V((rows, ff), BF16),
                V((ff, rows), BF16),
                V((members, tokens, chunk), BF16),
                V((mp, mloc, dp, tokens, chunk), BF16),
                V((dp, 2, 8, tokens), F32),
                V((dp, tokens, ff), F32),
                V((dp, ff // TILE, tokens, TILE), BF16),
                V((dp, dp - 1, ff // TILE, tokens, TILE), BF16),
                V((dp, tokens, ff), BF16),
                V((dp, tokens, half), F32),
                V((dp, half // TILE, tokens, TILE), BF16),
                V((dp, half // TILE, tokens, TILE), BF16),
                V((dp, nh, half // TILE, tokens, TILE), BF16),
                V((dp, tokens, half), BF16),
                V((dp, tokens, half), BF16),
                V((dp, 8, tokens), F32),
                V((dp, peers, 8, tokens), F32),
                V((dp, 8, LANES), F32),
                V((dp, tokens, rows), F32),
                V((dp, tokens, rows), BF16),
                V((dp, tokens, ff), F32),
                V((dp, ff // TILE, tokens, TILE), BF16),
                V((dp, tokens, ff), BF16),
                V((dp, nh, mloc, tokens, chunk), BF16),
                V((dp, nh, mloc, tokens, chunk), BF16),
                V((dp, nh, mloc, tokens, chunk), F32),
                V((dp, nh, mloc, tokens, chunk), BF16),
                V((dp, nh, mloc, tokens, chunk), BF16),
                V((dp, mloc, tokens, chunk), BF16),
                V((members, tokens, chunk), BF16),
                dma(2), dma(4), dma(sends), dma(members), dma(mp * mloc * dp), dma(dp),
                dma(dp * dp * (ff // TILE)), dma(dp * (half // TILE)),
                dma(dp * nh * (half // TILE)), dma(dp), dma(dp), dma(dp),
                dma(dp * dp * (ff // TILE)), dma(dp * nh), dma(dp * nh),
                dma(dp * mloc), dma(members),
            ],
            compiler_params=pltpu.CompilerParams(
                collective_id=0, has_side_effects=True, vmem_limit_bytes=60 * 2**20
            ),
            cost_estimate=pl.CostEstimate(
                flops=flops, bytes_accessed=4 * rows * ff, transcendentals=0
            ),
        )(lengths, reward_offset, seq_weight, hidden, score_vec, w_in, w_out)

        steps = mloc * mp
        out_rows = ff // steps
        whole = lambda *shape: pl.BlockSpec(shape, lambda i: (0,) * len(shape))
        gin, gout, pen, gh = pl.pallas_call(
            weight_kernel,
            grid=(steps,),
            out_shape=(sds((1, rows, ff), F32), sds((1, ff, rows), F32), sds((1, seqs), F32),
                       sds((tokens, chunk), F32)),
            in_specs=[
                pl.BlockSpec((1, 1, dp, tokens, chunk), lambda i: (i % mp, i // mp, 0, 0, 0)),
                whole(dp, tokens, ff),
                pl.BlockSpec((dp, tokens, out_rows), lambda i: (0, 0, i)),
                whole(dp, tokens, rows),
                whole(1, seqs),
                whole(tokens, chunk),
            ],
            out_specs=(
                pl.BlockSpec((1, chunk, ff), lambda i: (0, i, 0)),
                pl.BlockSpec((1, out_rows, rows), lambda i: (0, i, 0)),
                whole(1, seqs),
                whole(tokens, chunk),
            ),
            compiler_params=pltpu.CompilerParams(vmem_limit_bytes=60 * 2**20),
            cost_estimate=pl.CostEstimate(
                flops=flops // 2, bytes_accessed=8 * rows * ff, transcendentals=0
            ),
        )(h, bg, act, sh, pen, gh)
        return pen, gh, gin, gout

    in_specs = (
        P("dp", ("member", "mp")),
        P("member", "dp", "mp"),
        P("member", "mp", "dp"),
        P("member", None),
        P("dp", None),
        P("dp", None),
        P("dp", None),
    )
    out_specs = (
        P("dp", None),
        P("dp", ("member", "mp")),
        P("member", "dp", "mp"),
        P("member", "mp", "dp"),
    )
    return jax.shard_map(local, mesh=mesh, in_specs=in_specs, out_specs=out_specs, check_vma=False)
```

```python
import functools

import jax
import jax.numpy as jnp
from jax import lax
from jax.experimental import pallas as pl
from jax.experimental.pallas import tpu as pltpu
from jax.sharding import PartitionSpec as P

PENALTY = 0.5
SPREAD_FLOOR = 0.25
EPSILON = 1e-05
MESH = pl.DeviceIdType.MESH
ALONG = (((0,), (0,)), ((), ()))
F32 = jnp.float32
BF16 = jnp.bfloat16
LANES = 128
CORES = 2
TILE = 256


def dot(a, b):
    return jnp.dot(a, b, preferred_element_type=F32)


def sigmoid(v):
    return 1.0 / (1.0 + jnp.exp(-v))


def trunk_kernel(
    sizes,
    len_ref, off_ref, sw_ref, hid_ref, vec_ref, win_hbm, wout_hbm,
    pen_out, gh_out, h_out, act_out, sh_out, bg_out,
    win, wout, z, h, pool, gp, gs, gr, act, bp, bs, br, xr, cs, cr, ps, sc, pens,
    sf, sh, bk, ks, bg, fs, fr, fo, x2s, x2r, ts, zr, win_t, wout_t,
    local_sem, out_sem, send_sem, z_sem, h_sem, pool_sem, g_sem, b_sem, x_sem, c_sem,
    sc_send, sc_recv, k_sem, f_sem, x2_sem, t_send, t_recv,
):
    dp, members, mp, tokens, chunk, ff, seqs, features = sizes
    nh = mp // CORES
    mloc = members // dp
    half = mloc * mp * chunk // CORES
    d = lax.axis_index("dp")
    m = lax.axis_index("member")
    p = lax.axis_index("mp")
    hi = p // CORES
    lo = p % CORES
    sib = hi * CORES + (1 - lo)

    def device(dd, mm, pp):
        return {"dp": dd, "member": mm, "mp": pp}

    def hsem(q, j, s):
        return h_sem.at[(q * mloc + j) * dp + s]

    sent = []

    def push(src, dst, sem, to, now=True):
        copy = pltpu.make_async_remote_copy(
            src_ref=src, dst_ref=dst, send_sem=send_sem.at[len(sent)], recv_sem=sem,
            device_id=to, device_id_type=MESH,
        )
        if now:
            copy.start()
        sent.append(copy)
        return copy

    def arrived(ref, sem):
        pltpu.make_async_copy(ref, ref, sem).wait()

    load_in = pltpu.make_async_copy(win_hbm.at[0], win, local_sem.at[0])
    load_out = pltpu.make_async_copy(wout_hbm.at[0], wout, local_sem.at[1])
    load_in.start()
    load_out.start()

    group = [
        (a, b, c)
        for a in range(dp) for b in range(members) for c in range(CORES)
        if (a, b, c) != (0, 0, 0)
    ]

    def relative(a, b, c):
        return (
            lax.rem(d + a, dp), lax.rem(m + b, members), lax.rem(lo + c, CORES)
        )

    others_hi = [lax.rem(hi + r, nh) for r in range(1, nh)]
    others_d = [lax.rem(d + r, dp) for r in range(1, dp)]
    barrier = pltpu.get_barrier_semaphore()
    for a, b, c in group:
        dd, mm, cc = relative(a, b, c)
        pl.semaphore_signal(
            barrier, inc=1, device_id=device(dd, mm, hi * CORES + cc), device_id_type=MESH
        )
    for hh in others_hi:
        pl.semaphore_signal(
            barrier, inc=1, device_id=device(d, m, hh * CORES + lo), device_id_type=MESH
        )
    pl.semaphore_wait(barrier, len(group) + nh - 1)

    pltpu.make_async_copy(hid_ref, z.at[m], z_sem.at[m]).start()
    for r in range(1, members):
        push(hid_ref, z.at[m], z_sem.at[m], device(d, lax.rem(m + r, members), p))

    place = lax.broadcasted_iota(jnp.int32, (1, tokens), 1)
    row = lax.broadcasted_iota(jnp.int32, (8, tokens), 0)
    pooled = jnp.zeros((8, tokens), F32)
    weights = jnp.zeros((8, tokens), F32)
    start = jnp.int32(0)
    for i in range(seqs):
        size = len_ref[0, i]
        target = start + lax.rem(off_ref[0, i], size)
        inside = jnp.where((place >= start) & (place < start + size), 1.0, 0.0)
        value = inside / jnp.full((1, tokens), size, jnp.int32).astype(F32)
        value = value + jnp.where(place == target, 1.0, 0.0)
        pooled = jnp.where(row == i, value, pooled)
        weights = jnp.where(row == i, sw_ref[0, i], weights)
        start = start + size
    pool[d, 0] = pooled
    pool[d, 1] = weights
    for dd in others_d:
        push(pool.at[d], pool.at[d], pool_sem.at[d], device(dd, m, p))

    across, along_mp = [], []
    for dd in others_d:
        for j in range(mloc):
            c = dd * mloc + j
            across.append((c, [push(
                z.at[c], h.at[p, j, d], hsem(p, j, d), device(dd, m, p), False
            )]))
    for j in range(mloc):
        c = d * mloc + j
        copies = [
            push(z.at[c], h.at[p, j, d], hsem(p, j, d), device(d, m, to), False)
            for to in [hh * CORES + lo for hh in others_hi] + [sib]
        ]
        copies.append(pltpu.make_async_copy(z.at[c], h.at[p, j, d], hsem(p, j, d)))
        along_mp.append((c, copies))

    def forward(entries):
        for c, copies in entries:
            arrived(z.at[c], z_sem.at[c])
            for copy in copies:
                copy.start()

    near_own = m // mloc == d

    @pl.when(near_own)
    def _():
        forward(along_mp + across)

    @pl.when(jnp.logical_not(near_own))
    def _():
        forward(across + along_mp)

    for dd in others_d:
        for j in range(mloc):
            arrived(h.at[p, j, dd], hsem(p, j, dd))
            for hh in others_hi:
                push(h.at[p, j, dd], h.at[p, j, dd], hsem(p, j, dd), device(d, m, hh * CORES + lo))
            push(h.at[p, j, dd], h.at[p, j, dd], hsem(p, j, dd), device(d, m, sib))
    for j in range(mloc):
        arrived(h.at[p, j, d], hsem(p, j, d))

    def gate_rows(q, j):
        return pl.ds(pl.multiple_of((j * mp + q) * chunk, chunk), chunk)

    def gate_add(q, first):
        for c in range(0, ff, TILE):
            total = None
            for j in range(mloc):
                left = h[q, j].reshape(dp * tokens, chunk)
                term = dot(left, win[gate_rows(q, j), c:c + TILE])
                total = term if total is None else total + term
            total = total.reshape(dp, tokens, TILE)
            if not first:
                total = total + gp[:, :, c:c + TILE]
            gp[:, :, c:c + TILE] = total

    def all_here(q):
        for j in range(mloc):
            for s in range(dp):
                arrived(h.at[q, j, s], hsem(q, j, s))

    waited = []
    tiles = ff // TILE

    def tile_sem(sem, s, slot, t):
        return sem.at[(s * dp + slot) * tiles + t]

    def send_tile(src, s, t, sem):
        copies = []
        for k, dd in enumerate(others_d):
            slot = dp - 2 - k
            copies.append(push(
                src.at[s, t], gr.at[s, slot, t], tile_sem(sem, s, slot, t), device(dd, m, p)
            ))
        return copies

    def turn(src, dst):
        for a in range(0, src.shape[0], TILE):
            for b in range(0, src.shape[1], TILE):
                dst[b:b + TILE, a:a + TILE] = jnp.transpose(src[a:a + TILE, b:b + TILE])

    load_in.wait()
    gate_add(p, True)
    turn(win, win_t)
    all_here(sib)
    gate_add(sib, False)
    for hh in others_hi:
        q = hh * CORES + lo
        for j in range(mloc):
            for s in range(dp):
                arrived(h.at[q, j, s], hsem(q, j, s))
                push(h.at[q, j, s], h.at[q, j, s], hsem(q, j, s), device(d, m, sib))
        gate_add(q, False)
    for k, hh in enumerate(others_hi):
        q = hh * CORES + (1 - lo)
        all_here(q)
        if k < len(others_hi) - 1:
            gate_add(q, False)
            continue
        early = {}
        for s in range(dp):
            for t in range(ff // TILE):
                cols = slice(t * TILE, (t + 1) * TILE)
                total = gp[s, :, cols]
                for j in range(mloc):
                    total = total + dot(h[q, j, s], win[gate_rows(q, j), cols])
                gp[s, :, cols] = total
                gs[s, t] = total.astype(BF16)
                for copy in early.pop((s - 1, t), ()):
                    copy.wait_send()
                    waited.append(copy)
                early[s, t] = send_tile(gs, s, t, g_sem)
    keep_h = pltpu.make_async_copy(h, h_out, out_sem.at[0])
    keep_h.start()

    load_out.wait()
    turn(wout, wout_t)
    halves = half // TILE
    for s in range(dp):
        for t in range(tiles):
            cols = slice(t * TILE, (t + 1) * TILE)
            gate = gp[s, :, cols]
            for slot in range(dp - 1):
                arrived(gr.at[s, slot, t], tile_sem(g_sem, s, slot, t))
                gate = gate + gr[s, slot, t].astype(F32)
            gp[s, :, cols] = gate
            act[s, :, cols] = (gate * sigmoid(gate)).astype(BF16)
        for t in range(halves):
            cols = pl.ds(pl.multiple_of((1 - lo) * half + t * TILE, TILE), TILE)
            bs[s, t] = dot(act[s], wout[:, cols]).astype(BF16)
            push(bs.at[s, t], br.at[s, t], b_sem.at[s * halves + t], device(d, m, sib))
        for t in range(halves):
            cols = pl.ds(pl.multiple_of(lo * half + t * TILE, TILE), TILE)
            term = dot(act[s], wout[:, cols])
            arrived(br.at[s, t], b_sem.at[s * halves + t])
            xr[s, hi, t] = (term + br[s, t].astype(F32)).astype(BF16)
            for hh in others_hi:
                push(
                    xr.at[s, hi, t], xr.at[s, hi, t], x_sem.at[(s * nh + hi) * halves + t],
                    device(d, m, hh * CORES + lo),
                )
    keep_act = pltpu.make_async_copy(act, act_out, out_sem.at[1])
    keep_act.start()

    lane = lax.broadcasted_iota(jnp.int32, (tokens, LANES), 1)

    def combine(s):
        squares = jnp.zeros((tokens, 1), F32)
        along = jnp.zeros((tokens, 1), F32)
        per = TILE // chunk
        for k in range(half // chunk):
            block = lo * (half // chunk) + k
            c = k * chunk
            t, inner = k // per, slice(k % per * chunk, (k % per + 1) * chunk)
            if k % per == 0:
                for hh in others_hi:
                    arrived(xr.at[s, hh, t], x_sem.at[(s * nh + hh) * halves + t])
            branch = xr[s, 0, t, :, inner].astype(F32)
            for hh in range(1, nh):
                branch = branch + xr[s, hh, t, :, inner].astype(F32)
            comb = h[block % mp, block // mp, s].astype(F32) + branch
            bp[s, :, c:c + chunk] = comb
            cs[s, :, c:c + chunk] = comb.astype(BF16)
            cols = pl.ds(pl.multiple_of((d * CORES + lo) * half + c, chunk), chunk)
            squares = squares + jnp.sum(comb * comb, axis=1, keepdims=True)
            along = along + jnp.sum(comb * vec_ref[:, cols], axis=1, keepdims=True)
        both = jnp.where(lane == 0, squares, along)
        ps[s] = jnp.transpose(both)[:8]
        mine = (m * dp + d) * CORES + lo
        pltpu.make_async_copy(ps.at[s], sc.at[s, mine], sc_recv.at[s]).start()
        for a, b, c in group:
            dd, mm, cc = relative(a, b, c)
            pltpu.make_async_remote_copy(
                src_ref=ps.at[s], dst_ref=sc.at[s, mine],
                send_sem=sc_send.at[s], recv_sem=sc_recv.at[s],
                device_id=device(dd, mm, hi * CORES + cc), device_id_type=MESH,
            ).start()
        push(cs.at[s], cr.at[s], c_sem.at[s], device(d, m, sib))

    def slopes_of(s):
        arrived(sc.at[s], sc_recv.at[s])
        pooled = pool[s, 0]

        def head(mm):
            total = sc[s, mm * dp * CORES]
            for i in range(1, dp * CORES):
                total = total + sc[s, mm * dp * CORES + i]
            inv = lax.rsqrt(total[0:1] / features + EPSILON)
            score = total[1:2] * inv
            return inv, score, jnp.sum(score * pooled, axis=1, keepdims=True)

        rewards = [head(mm)[2] for mm in range(members)]
        center = rewards[0]
        for mm in range(1, members):
            center = center + rewards[mm]
        center = center / members
        spread = (rewards[0] - center) ** 2
        for mm in range(1, members):
            spread = spread + (rewards[mm] - center) ** 2
        deviation = jnp.sqrt(spread / members + SPREAD_FLOOR)
        pens[s] = jnp.broadcast_to(center - PENALTY * deviation, (8, LANES))
        inv, score, reward = head(m)
        pull = pool[s, 1] * (1.0 - PENALTY * (reward - center) / deviation) / members
        weight = jnp.sum(pooled * pull, axis=0, keepdims=True)
        by_vec = weight * inv
        by_comb = weight * (score * inv * inv / features)
        rows = lax.broadcasted_iota(jnp.int32, (LANES, tokens), 0)
        both = jnp.transpose(jnp.where(rows == 0, by_vec, by_comb))
        by_vec, by_comb = both[:, 0:1], both[:, 1:2]
        arrived(cr.at[s], c_sem.at[s])
        for own in (True, False):
            base = lo * half if own else (1 - lo) * half
            for c in range(0, half, TILE):
                comb = bp[s, :, c:c + TILE] if own else cr[s, :, c:c + TILE].astype(F32)
                vec = vec_ref[:, pl.ds(pl.multiple_of(d * CORES * half + base + c, TILE), TILE)]
                slope = by_vec * vec - by_comb * comb
                cols = pl.ds(pl.multiple_of(base + c, TILE), TILE)
                sf[s, :, cols] = slope
                sh[s, :, cols] = slope.astype(BF16)
        for t in range(tiles):
            cols = slice(t * TILE, (t + 1) * TILE)
            term = dot(sh[s], wout_t[:, cols])
            bk[s, :, cols] = term
            ks[s, t] = term.astype(BF16)
            send_tile(ks, s, t, k_sem)

    for dd in others_d:
        arrived(pool.at[dd], pool_sem.at[dd])
    for s in range(dp):
        combine(s)
        slopes_of(s)
    keep_sh = pltpu.make_async_copy(sh, sh_out, out_sem.at[2])
    keep_sh.start()
    spot = lax.broadcasted_iota(jnp.int32, (8, LANES), 1)
    diag = lax.broadcasted_iota(jnp.int32, (8, LANES), 0) == spot
    flat = jnp.sum(jnp.where(diag, pens[d], 0.0), axis=0, keepdims=True)
    pen_out[...] = flat[:, :seqs]

    last = []

    def finish(s):
        arrived(fr.at[s, hi], f_sem.at[s * nh + hi])
        for hh in others_hi:
            arrived(x2r.at[s, hh], x2_sem.at[s * nh + hh])
        for j in range(mloc):
            total = fo[s, hi, j] + fr[s, hi, j].astype(F32)
            for hh in others_hi:
                total = total + x2r[s, hh, j].astype(F32)
            cols = pl.ds(pl.multiple_of((j * mp + p) * chunk, chunk), chunk)
            ts[s, j] = (total + sf[s, :, cols]).astype(BF16)
            to = d * mloc + j
            here = jnp.logical_and(d == s, to == m)
            away = pltpu.make_async_remote_copy(
                src_ref=ts.at[s, j], dst_ref=zr.at[m],
                send_sem=t_send.at[s * mloc + j], recv_sem=t_recv.at[m],
                device_id=device(jnp.int32(s), to, p), device_id_type=MESH,
            )
            near = pltpu.make_async_copy(ts.at[s, j], zr.at[m], t_recv.at[m])

            @pl.when(here)
            def _(near=near):
                near.start()

            @pl.when(jnp.logical_not(here))
            def _(away=away):
                away.start()

            last.append((here, away))

    for s in range(dp):
        for t in range(tiles):
            cols = slice(t * TILE, (t + 1) * TILE)
            raw = bk[s, :, cols]
            for slot in range(dp - 1):
                arrived(gr.at[s, slot, t], tile_sem(k_sem, s, slot, t))
                raw = raw + gr[s, slot, t].astype(F32)
            gate = gp[s, :, cols]
            sig = sigmoid(gate)
            bg[s, :, cols] = (raw * (sig * (1.0 + gate * (1.0 - sig)))).astype(BF16)

        def hidden_term(hh, j, cc):
            first = (j * mp + hh * CORES + cc) * chunk
            return dot(bg[s], win_t[:, pl.ds(pl.multiple_of(first, chunk), chunk)])

        for hh in others_hi + [hi]:
            for j in range(mloc):
                fs[s, hh, j] = hidden_term(hh, j, 1 - lo).astype(BF16)
            push(fs.at[s, hh], fr.at[s, hh], f_sem.at[s * nh + hh], device(d, m, sib))
            for j in range(mloc):
                fo[s, hh, j] = hidden_term(hh, j, lo)
            if hh is hi:
                continue
            arrived(fr.at[s, hh], f_sem.at[s * nh + hh])
            x2s[s, hh] = (fo[s, hh] + fr[s, hh].astype(F32)).astype(BF16)
            push(x2s.at[s, hh], x2r.at[s, hi], x2_sem.at[s * nh + hi], device(d, m, hh * CORES + lo))
        if s > 0:
            finish(s - 1)
    keep_bg = pltpu.make_async_copy(bg, bg_out, out_sem.at[3])
    keep_bg.start()
    finish(dp - 1)

    for mm in range(members):
        arrived(zr.at[mm], t_recv.at[mm])
    total = zr[0].astype(F32)
    for mm in range(1, members):
        total = total + zr[mm].astype(F32)
    gh_out[...] = total

    for copy in sent:
        if all(copy is not done for done in waited):
            copy.wait_send()
    for here, away in last:
        @pl.when(jnp.logical_not(here))
        def _(away=away):
            away.wait_send()
    for s in range(dp):
        some = sc.at[s, pl.ds(0, len(group))]
        pltpu.make_async_copy(some, some, sc_send.at[s]).wait()
    for copy in (keep_h, keep_act, keep_sh, keep_bg):
        copy.wait()


def weight_kernel(
    h_ref, bg_ref, act_ref, sh_ref, pen_ref, gh_ref, gin_ref, gout_ref, pen_out, gh_out
):
    pen_out[...] = pen_ref[...]
    gh_out[...] = gh_ref[...]

    def flat(ref):
        value = ref[...]
        return value.reshape(value.shape[-3] * value.shape[-2], value.shape[-1])

    def product(left, right):
        return lax.dot_general(left, right, ALONG, preferred_element_type=F32)

    gin_ref[0] = product(flat(h_ref), flat(bg_ref))
    gout_ref[0] = product(flat(act_ref), flat(sh_ref))


def solution(mesh):
    dp, members, mp = mesh.shape["dp"], mesh.shape["member"], mesh.shape["mp"]

    def local(hidden, w_in, w_out, score_vec, lengths, reward_offset, seq_weight):
        tokens, chunk = hidden.shape
        _, rows, ff = w_in.shape
        seqs = lengths.shape[1]
        features = score_vec.shape[1]
        nh = mp // CORES
        mloc = members // dp
        half = rows // CORES
        peers = dp * members * CORES
        sizes = (dp, members, mp, tokens, chunk, ff, seqs, features)
        smem = pl.BlockSpec(memory_space=pltpu.SMEM)
        vmem = pl.BlockSpec(memory_space=pltpu.VMEM)
        hbm = pl.BlockSpec(memory_space=pl.ANY)
        V = pltpu.VMEM
        dma = lambda n: pltpu.SemaphoreType.DMA((n,))
        sds = jax.ShapeDtypeStruct
        sends = 64 + 16 * dp + 2 * dp * dp * (ff // TILE)
        flops = 8 * dp * tokens * rows * ff
        pen, gh, h, act, sh, bg = pl.pallas_call(
            functools.partial(trunk_kernel, sizes),
            out_shape=(
                sds((1, seqs), F32),
                sds((tokens, chunk), F32),
                sds((mp, mloc, dp, tokens, chunk), BF16),
                sds((dp, tokens, ff), BF16),
                sds((dp, tokens, rows), BF16),
                sds((dp, tokens, ff), BF16),
            ),
            in_specs=[smem, smem, smem, hbm, vmem, hbm, hbm],
            out_specs=(vmem, vmem, hbm, hbm, hbm, hbm),
            scratch_shapes=[
                V((rows, ff), BF16),
                V((ff, rows), BF16),
                V((members, tokens, chunk), BF16),
                V((mp, mloc, dp, tokens, chunk), BF16),
                V((dp, 2, 8, tokens), F32),
                V((dp, tokens, ff), F32),
                V((dp, ff // TILE, tokens, TILE), BF16),
                V((dp, dp - 1, ff // TILE, tokens, TILE), BF16),
                V((dp, tokens, ff), BF16),
                V((dp, tokens, half), F32),
                V((dp, half // TILE, tokens, TILE), BF16),
                V((dp, half // TILE, tokens, TILE), BF16),
                V((dp, nh, half // TILE, tokens, TILE), BF16),
                V((dp, tokens, half), BF16),
                V((dp, tokens, half), BF16),
                V((dp, 8, tokens), F32),
                V((dp, peers, 8, tokens), F32),
                V((dp, 8, LANES), F32),
                V((dp, tokens, rows), F32),
                V((dp, tokens, rows), BF16),
                V((dp, tokens, ff), F32),
                V((dp, ff // TILE, tokens, TILE), BF16),
                V((dp, tokens, ff), BF16),
                V((dp, nh, mloc, tokens, chunk), BF16),
                V((dp, nh, mloc, tokens, chunk), BF16),
                V((dp, nh, mloc, tokens, chunk), F32),
                V((dp, nh, mloc, tokens, chunk), BF16),
                V((dp, nh, mloc, tokens, chunk), BF16),
                V((dp, mloc, tokens, chunk), BF16),
                V((members, tokens, chunk), BF16),
                V((ff, rows), BF16),
                V((rows, ff), BF16),
                dma(2), dma(4), dma(sends), dma(members), dma(mp * mloc * dp), dma(dp),
                dma(dp * dp * (ff // TILE)), dma(dp * (half // TILE)),
                dma(dp * nh * (half // TILE)), dma(dp), dma(dp), dma(dp),
                dma(dp * dp * (ff // TILE)), dma(dp * nh), dma(dp * nh),
                dma(dp * mloc), dma(members),
            ],
            compiler_params=pltpu.CompilerParams(
                collective_id=0, has_side_effects=True, vmem_limit_bytes=60 * 2**20
            ),
            cost_estimate=pl.CostEstimate(
                flops=flops, bytes_accessed=4 * rows * ff, transcendentals=0
            ),
        )(lengths, reward_offset, seq_weight, hidden, score_vec, w_in, w_out)

        steps = mloc * mp
        out_rows = ff // steps
        whole = lambda *shape: pl.BlockSpec(shape, lambda i: (0,) * len(shape))
        gin, gout, pen, gh = pl.pallas_call(
            weight_kernel,
            grid=(steps,),
            out_shape=(sds((1, rows, ff), F32), sds((1, ff, rows), F32), sds((1, seqs), F32),
                       sds((tokens, chunk), F32)),
            in_specs=[
                pl.BlockSpec((1, 1, dp, tokens, chunk), lambda i: (i % mp, i // mp, 0, 0, 0)),
                whole(dp, tokens, ff),
                pl.BlockSpec((dp, tokens, out_rows), lambda i: (0, 0, i)),
                whole(dp, tokens, rows),
                whole(1, seqs),
                whole(tokens, chunk),
            ],
            out_specs=(
                pl.BlockSpec((1, chunk, ff), lambda i: (0, i, 0)),
                pl.BlockSpec((1, out_rows, rows), lambda i: (0, i, 0)),
                whole(1, seqs),
                whole(tokens, chunk),
            ),
            compiler_params=pltpu.CompilerParams(vmem_limit_bytes=60 * 2**20),
            cost_estimate=pl.CostEstimate(
                flops=flops // 2, bytes_accessed=8 * rows * ff, transcendentals=0
            ),
        )(h, bg, act, sh, pen, gh)
        return pen, gh, gin, gout

    in_specs = (
        P("dp", ("member", "mp")),
        P("member", "dp", "mp"),
        P("member", "mp", "dp"),
        P("member", None),
        P("dp", None),
        P("dp", None),
        P("dp", None),
    )
    out_specs = (
        P("dp", None),
        P("dp", ("member", "mp")),
        P("member", "dp", "mp"),
        P("member", "mp", "dp"),
    )
    return jax.shard_map(local, mesh=mesh, in_specs=in_specs, out_specs=out_specs, check_vma=False)
```
